512 devices in a mesh: tile: 128 (over x, z, core), chan: 4 (over y).
Axes of the slice: x: 4, y: 4, z: 16, core: 2. Of those that a mesh axis runs over, the one named last changes fastest.
Arguments:
- atm_state: bfloat16 [256, 131072], P('chan', 'tile'), may hold values from -6 to 6
- ocean_state: bfloat16 [128, 131072], P('chan', 'tile'), may hold values from -6 to 6
- conv_weight: bfloat16 [9, 384, 256], replicated, may hold values from -0.109375 to 0.109375
- conv_bias: float32 [256], P('chan'), may hold values from -3 to 3
- regrid_weight: bfloat16 [1536, 128, 128], P('tile'), may hold values from 0 to 0.25
- out_grad: bfloat16 [256, 131072], P('chan', 'tile'), may hold values from -6 to 6
- atm_neighbours: int32 [128, 8], P('tile'), may hold values from -1 to 127, as said below
- coupling_sources: int32 [128, 4], P('tile'), may hold values from 0 to 127, as said below
- coupling_blocks: int32 [128, 12], P('tile'), may hold values from -1 to 7, as said below
- coupling_sends: int32 [128, 128, 3], P('tile'), may hold values from -1 to 7, as said below
Outputs:
- atm_output: bfloat16 [256, 131072], P('chan', 'tile')
- atm_input_grad: bfloat16 [256, 131072], P('chan', 'tile')
- ocean_grad: float32 [128, 131072], P('chan', 'tile')
- weight_grad: float32 [9, 384, 256], P(None, None, 'chan')
- bias_grad: float32 [256], P('chan')
The draws below stay inside these ranges and needn't reach their ends.
Inputs may be any that keep to these rules, and one draw needn't show every extreme that they name: `atm_neighbours`: devices 8 * r to 8 * r + 7 hold the patches of row r of a grid of patches with 8 columns, in an order drawn from the seed; an entry names the device of the adjacent patch in that direction, -1 beyond the grid's edge; if device d names p in a direction, p names d in the opposite one. `coupling_sources`: the 4 sources of device p are different and differ from p + 128 / 2 by at most 3 modulo 128; the first source is p + 128 / 2 modulo 128. `coupling_blocks`: -1 marks an entry over land; the entries of the first source are never -1; in every draw some device has all 12 entries live. coupling_sends[q, p, c] is not -1 exactly where some entry k * 3 + c of device p has source q and is live.
All inputs are finite; a program needn't handle non-finite values.
Results may differ from the reference program's by a relative error of at most 0.008.
Values may be sent and summed in bfloat16 or wider, within the bound.
No kernel may reach another device: no remote copies, remote signals or barrier semaphores. Data moves between devices by JAX's collectives and lax.ppermute only.
A program may use at most 64 MiB of HBM per device.

```python
import math
import jax
import jax.numpy as jnp
from jax import lax

CA = 256
CO = 128
KIN = 384
SC = 128
SR = 8
PATCH_COLS = 8
OBLK = 8
ABLK = 8
NSRC = 4
CAP = 3
SPAN = 3
NE = 12
ATM_CELLS = 131072
OCN_CELLS = 131072
N_TILE = 128


DIRECTIONS = ((-1, 0), (1, 0), (0, -1), (0, 1), (-1, -1), (-1, 1), (1, -1), (1, 1))


def coupling_tables(key):
    key = jax.random.fold_in(key, 7)
    key_offsets, key_level, key_live, key_atm, key_ocean, key_full = jax.random.split(key, 6)
    offset_keys = jax.random.split(key_offsets, N_TILE)
    orders = jax.vmap(lambda subkey: jax.random.permutation(subkey, 2 * SPAN))(offset_keys).astype(jnp.int32)
    others = orders[:, :NSRC - 1]
    others = jnp.where(others < SPAN, others - SPAN, others - SPAN + 1)
    devices = jnp.arange(N_TILE, dtype=jnp.int32)
    offsets = jnp.concatenate([jnp.zeros((N_TILE, 1), jnp.int32), others], axis=1)
    sources = (devices[:, None] + N_TILE // 2 + offsets) % N_TILE
    land_level = jax.random.randint(key_level, (N_TILE, 1), 2, 9)
    busiest = jax.random.randint(key_full, (), 0, N_TILE)
    land_level = jnp.where(devices[:, None] == busiest, 8, land_level)
    entry_ids = jnp.arange(NE, dtype=jnp.int32)[None, :]
    wet_entry = (jax.random.randint(key_live, (N_TILE, NE), 0, 8) < land_level) | (entry_ids < CAP)
    atm_blocks = jnp.where(wet_entry, jax.random.randint(key_atm, (N_TILE, NE), 0, ABLK), -1).astype(jnp.int32)
    ocean_blocks = jnp.where(wet_entry, jax.random.randint(key_ocean, (N_TILE, NE), 0, OBLK), -1).astype(jnp.int32)
    entry_src = jnp.repeat(sources, CAP, axis=1)
    entry_slot = jnp.tile(jnp.arange(CAP, dtype=jnp.int32), NSRC)[None, :] + 0 * entry_src
    receiver = devices[:, None] + 0 * entry_src
    send_table = jnp.full((N_TILE, N_TILE, CAP), -1, jnp.int32).at[entry_src, receiver, entry_slot].set(ocean_blocks)
    return (sources.astype(jnp.int32), atm_blocks, send_table)


def draw_coupling_sources(key, part):
    return coupling_tables(key)[0]


def draw_coupling_blocks(key, part):
    return coupling_tables(key)[1]


def draw_coupling_sends(key, part):
    return coupling_tables(key)[2]


def draw_atm_neighbours(key, part):
    key = jax.random.fold_in(key, 11)
    grid_rows = N_TILE // PATCH_COLS
    row_orders = jax.vmap(lambda subkey: jax.random.permutation(subkey, PATCH_COLS))(jax.random.split(key, grid_rows)).astype(jnp.int32)
    device_of = jnp.arange(grid_rows, dtype=jnp.int32)[:, None] * PATCH_COLS + row_orders
    padded = jnp.pad(device_of, 1, constant_values=-1)
    column_of = jnp.argsort(row_orders, axis=1, stable=True).reshape(N_TILE).astype(jnp.int32)
    row_index = jnp.arange(N_TILE, dtype=jnp.int32) // PATCH_COLS
    return jnp.stack([padded[row_index + 1 + step_row, column_of + 1 + step_col] for step_row, step_col in DIRECTIONS], axis=1).astype(jnp.int32)


def shard_levels(key, shape, shards, low, top_value):
    loudness, own = 1.0, jax.random.fold_in(key, 6)
    for axis_at, parts in shards:
        draws = jnp.exp(jax.random.uniform(jax.random.fold_in(own, axis_at), (parts,), jnp.float32, low / len(shards), top_value / len(shards)))
        loudness = loudness * jnp.repeat(draws, shape[axis_at] // parts).reshape([-1 if axis == axis_at else 1 for axis in range(len(shape))])
    return loudness


def scatter_about(rng, shape, spread, bound, cuts=(), held_as=jnp.bfloat16):
    drawn = jax.random.normal(rng, shape, jnp.float32) * spread
    if len(cuts) > 0:
        drawn = shard_levels(rng, shape, cuts, -0.22, 0.18) * drawn
    return jnp.clip(drawn, min=-bound, max=bound).astype(held_as)


def setup_inputs(seed: int = 0) -> dict:
    keys = jax.random.split(jax.random.key(seed), 11)
    return {
        "atm_state": scatter_about(keys[0], (CA, ATM_CELLS), 1.0, 6.0, ((0, 4), (1, 128))),
        "ocean_state": scatter_about(keys[1], (CO, OCN_CELLS), 1.0, 6.0, ((0, 4), (1, 128))),
        "conv_weight": scatter_about(keys[2], (9, KIN, CA), (9 * KIN) ** -0.5, 0.109375),
        "conv_bias": scatter_about(keys[3], (CA,), 0.5, 3.0, ((0, 4),), jnp.float32),
        "regrid_weight": jnp.clip(0.25 * jax.random.uniform(keys[4], (N_TILE * NE, 128, 128), jnp.float32) ** shard_levels(keys[4], (N_TILE * NE, 128, 128), ((0, 128),), -0.2, 0.2), 0.0, 0.25).astype(jnp.bfloat16),
        "out_grad": scatter_about(keys[5], (CA, ATM_CELLS), 1.0, 6.0, ((0, 4), (1, 128))),
        "atm_neighbours": draw_atm_neighbours(jax.random.fold_in(keys[10], 71), 0),
        "coupling_sources": draw_coupling_sources(jax.random.fold_in(keys[10], 71), 0),
        "coupling_blocks": draw_coupling_blocks(jax.random.fold_in(keys[10], 71), 0),
        "coupling_sends": draw_coupling_sends(jax.random.fold_in(keys[10], 71), 0),
    }


OPPOSITE = (1, 0, 3, 2, 7, 6, 5, 4)
SIDE_OF = (0, 1, 2, 3, 0, 0, 1, 1)
OFFSETS = ((-1, -1), (-1, 0), (-1, 1), (0, -1), (0, 0), (0, 1), (1, -1), (1, 0), (1, 1))
PRECISE = lax.Precision.HIGHEST

def make_strips(surface):
    height = surface.shape[1]
    columns = surface.shape[2]
    west_col = jnp.pad(surface[:, :, 0], ((0, 0), (0, columns - height)))
    east_col = jnp.pad(surface[:, :, columns - 1], ((0, 0), (0, columns - height)))
    side_rows = (surface[:, 0, :], surface[:, height - 1, :], west_col, east_col)
    return jnp.stack([side_rows[side] for side in SIDE_OF], axis=0)

def pad_patch(surface, arrived):
    height = surface.shape[1]
    columns = surface.shape[2]
    north_row = jnp.concatenate([arrived[4][:, columns - 1:], arrived[0], arrived[5][:, :1]], axis=1)
    south_row = jnp.concatenate([arrived[6][:, columns - 1:], arrived[1], arrived[7][:, :1]], axis=1)
    central = jnp.concatenate([arrived[2][:, :height, None], surface, arrived[3][:, :height, None]], axis=2)
    return jnp.concatenate([north_row[:, None], central, south_row[:, None]], axis=1)

def halo_all(surfaces, neighbours):
    strips_out = jax.vmap(make_strips)(surfaces)
    facing = jnp.array(OPPOSITE, dtype=jnp.int32)
    arrived = strips_out[jnp.maximum(neighbours, 0), facing[None, :]]
    arrived = jnp.where((neighbours >= 0)[:, :, None, None], arrived, jnp.zeros((), surfaces.dtype))
    return jax.vmap(pad_patch)(surfaces, arrived)

def window(padded, shift_row, shift_col):
    channels = padded.shape[0]
    return padded[:, 1 + shift_row:1 + shift_row + SR, 1 + shift_col:1 + shift_col + SC].reshape(channels, SR * SC)

def reference(atm_state, ocean_state, conv_weight, conv_bias, regrid_weight, out_grad, atm_neighbours, coupling_sources, coupling_blocks, coupling_sends):
    tile_count = atm_neighbours.shape[0]
    device_ids = jnp.arange(tile_count, dtype=jnp.int32)
    entry_slot = jnp.tile(jnp.arange(CAP, dtype=jnp.int32), NSRC)
    entry_src = jnp.repeat(coupling_sources, CAP, axis=1)
    ocean_blocks = ocean_state.reshape(CO, tile_count, OBLK, 128)
    block_ids = jnp.arange(ABLK, dtype=jnp.int32)

    def to_patches(values):
        return values.reshape(values.shape[0], tile_count, SR, SC).transpose(1, 0, 2, 3)

    def from_patches(values):
        return values.transpose(1, 0, 2, 3).reshape(values.shape[1], tile_count * SR * SC)

    def regrid_one(device):
        sources = entry_src[device]
        chosen = coupling_sends[sources, device, entry_slot]
        picked = ocean_blocks[:, sources, jnp.maximum(chosen, 0)]
        picked = jnp.where((chosen >= 0)[None, :, None], picked, jnp.zeros((), picked.dtype))
        weights = lax.dynamic_slice_in_dim(regrid_weight, device * NE, NE, 0)
        block_terms = jnp.einsum('kes,est->ekt', picked.astype(jnp.float32), weights.astype(jnp.float32), precision=PRECISE)
        placement = (coupling_blocks[device][:, None] == block_ids[None, :]).astype(jnp.float32)
        summed = jnp.einsum('ea,ekt->kat', placement, block_terms, precision=PRECISE)
        return summed.reshape(CO, SR, SC).astype(jnp.bfloat16)
    regridded = lax.map(regrid_one, device_ids)
    atm_patches = to_patches(atm_state)
    grad_patches = to_patches(out_grad)
    padded_atm = halo_all(atm_patches, atm_neighbours)
    padded_ocean = halo_all(regridded, atm_neighbours)

    def forward_one(patch_items):
        pad_atm, pad_ocean, surface, grad_surface = patch_items
        total_sum = jnp.zeros((CA, SR * SC), jnp.float32)
        for offset in range(9):
            shift_row, shift_col = OFFSETS[offset]
            total_sum = total_sum + jnp.dot(conv_weight[offset, :CA].T, window(pad_atm, shift_row, shift_col), preferred_element_type=jnp.float32)
            total_sum = total_sum + jnp.dot(conv_weight[offset, CA:].T, window(pad_ocean, shift_row, shift_col), preferred_element_type=jnp.float32)
        pre_act = total_sum.reshape(CA, SR, SC) + conv_bias[:, None, None]
        sigmoid_z = jax.nn.sigmoid(pre_act)
        output = (surface.astype(jnp.float32) + pre_act * sigmoid_z).astype(jnp.bfloat16)
        z_grad = (grad_surface.astype(jnp.float32) * sigmoid_z * (1.0 + pre_act * (1.0 - sigmoid_z))).astype(jnp.bfloat16)
        return (output, z_grad)
    outputs, z_grads = lax.map(forward_one, (padded_atm, padded_ocean, atm_patches, grad_patches))
    padded_grad = halo_all(z_grads, atm_neighbours)

    def backward_one(patch_items):
        pad_grad, grad_surface = patch_items
        sum_atm = jnp.zeros((CA, SR * SC), jnp.float32)
        sum_ocean = jnp.zeros((CO, SR * SC), jnp.float32)
        for offset in range(9):
            shift_row, shift_col = OFFSETS[offset]
            grad_window = window(pad_grad, -shift_row, -shift_col)
            sum_atm = sum_atm + jnp.dot(conv_weight[offset, :CA], grad_window, preferred_element_type=jnp.float32)
            sum_ocean = sum_ocean + jnp.dot(conv_weight[offset, CA:], grad_window, preferred_element_type=jnp.float32)
        input_grad = (grad_surface.reshape(CA, SR * SC).astype(jnp.float32) + sum_atm).astype(jnp.bfloat16)
        return (input_grad.reshape(CA, SR, SC), sum_ocean.astype(jnp.bfloat16))
    input_grads, regrid_grads = lax.map(backward_one, (padded_grad, grad_patches))

    def return_one(device):
        placement = (coupling_blocks[device][:, None] == block_ids[None, :]).astype(jnp.float32)
        block_delta = regrid_grads[device].reshape(CO, ABLK, 128).astype(jnp.float32)
        taken_rows = jnp.einsum('ea,kas->eks', placement, block_delta, precision=PRECISE)
        weights = lax.dynamic_slice_in_dim(regrid_weight, device * NE, NE, 0)
        return jnp.einsum('ekt,est->eks', taken_rows, weights.astype(jnp.float32), precision=PRECISE).astype(jnp.bfloat16)
    return_terms = lax.map(return_one, device_ids)
    chosen_all = coupling_sends[entry_src, device_ids[:, None], entry_slot[None, :]]
    target = jnp.where(chosen_all >= 0, chosen_all, OBLK)
    grad_blocks = jnp.zeros((tile_count, OBLK + 1, CO, 128), jnp.float32).at[entry_src, target].add(return_terms.astype(jnp.float32))
    ocean_grad = grad_blocks[:, :OBLK].transpose(2, 0, 1, 3).reshape(CO, tile_count * OBLK * 128)

    def weight_step(running, patch_items):
        pad_atm, pad_ocean, z_grad = patch_items
        grad_cells = z_grad.reshape(CA, SR * SC)
        pieces = []
        for offset in range(9):
            shift_row, shift_col = OFFSETS[offset]
            pieces.append(jnp.concatenate([jnp.dot(window(pad_atm, shift_row, shift_col), grad_cells.T, preferred_element_type=jnp.float32), jnp.dot(window(pad_ocean, shift_row, shift_col), grad_cells.T, preferred_element_type=jnp.float32)], axis=0))
        return (running + jnp.stack(pieces, axis=0), None)
    weight_total, unused_out = lax.scan(weight_step, jnp.zeros((9, KIN, CA), jnp.float32), (padded_atm, padded_ocean, z_grads))
    grad_scale = 1.0 / math.sqrt(tile_count * SR * SC)
    bias_total = lax.optimization_barrier(jnp.sum(z_grads.astype(jnp.float32), axis=(0, 2, 3)))
    return (from_patches(outputs), from_patches(input_grads), ocean_grad, weight_total * grad_scale, bias_total * grad_scale)
```

```python
import functools
import math

import jax
import jax.numpy as jnp
import numpy as np
from jax import lax
from jax.experimental import pallas as pl
from jax.experimental.pallas import tpu as pltpu
from jax.sharding import PartitionSpec as P

BF, F32 = jnp.bfloat16, jnp.float32
TILES = 128
HALF = TILES // 2
LANES = 128
OG0, OC0, BIAS0 = 48, 68, 92
VMEM = pl.BlockSpec(memory_space=pltpu.VMEM)
SMEM = pl.BlockSpec(memory_space=pltpu.SMEM)

CHIP_STEPS = (-1, 0, 1)
ROW_CHIPS = [[8 * r + 2 * i + c for i in range(4)] for r in range(16) for c in range(2)]
SAME_CORE = [[2 * i + c for i in range(64)] for c in range(2)]


def one_hot(shape, pairs):
    table = np.zeros(shape, np.float32)
    for at in pairs:
        table[at] = 1.0
    return table.astype(jnp.bfloat16)


def edge_tables():
    atm = [(128 * (l // 2) + l % 2, l) for l in range(16)]
    atm += [(128 * (l // 2) + 126 + l % 2, 16 + l) for l in range(16)]
    grad = [(128 * r, 32 + r) for r in range(8)] + [(128 * r + 127, 40 + r) for r in range(8)]
    ocean = [(cell, lane + 64) for cell, lane in atm]
    return np.stack([one_hot((1024, 128), pairs) for pairs in (atm, grad, ocean)])


def corner_tables():
    tables = []
    for south in (0, 1):
        for east in (0, 1):
            first = 10 if south else 0
            near = 9 if south else 0
            col = 0 if east else 126
            both = [(128 * q + col + j, 4 * (first + q) + 2 * east + j) for q in (0, 1) for j in (0, 1)]
            both.append((256 + (0 if east else 127), OG0 + 2 * near + east))
            parts = [both]
            for q in (0, 1):
                parts.append([(384 + col + j, OC0 + 2 * (first + q) + j) for j in (0, 1)])
            tables.append(np.stack([one_hot((512, 128), pairs) for pairs in parts]))
    return np.stack(tables)


def beside_tables():
    tables = []
    for east in (0, 1):
        given = 0 if east else 16
        both = [(given + 2 * i + j, 4 * (i + 2) + 2 * east + j) for i in range(8) for j in (0, 1)]
        both += [((32 if east else 40) + i, OG0 + 2 * (i + 1) + east) for i in range(8)]
        ocean = [(64 + given + 2 * i + j, OC0 + 2 * (i + 2) + j) for i in range(8) for j in (0, 1)]
        tables.append(np.stack([one_hot((128, 128), pairs) for pairs in (both, ocean)]))
    return np.stack(tables)


def shift_tables():
    back = one_hot((128, 128), [(j - 1, j) for j in range(1, 128)])
    ahead = one_hot((128, 128), [(j + 1, j) for j in range(127)])
    return np.stack([back, ahead])


def input_side_tables():
    west = one_hot((128, 128 * 12), [(4 * r + 1, 128 * r) for r in range(12)])
    east = one_hot((128, 128 * 12), [(4 * r + 2, 128 * r + 127) for r in range(12)])
    gather = [(1536 + l, l) for l in range(48)]
    gather += [(128 * r + 127 * w, 48 + 2 * r + w) for r in range(12) for w in (0, 1)]
    taps = []
    for s in (-1, 0, 1):
        for t in (-1, 0, 1):
            at = 128 * (3 * (s + 1) + t + 1)
            for i in range(-1, 9):
                for w in (0, 1):
                    r = i + s + 2
                    col = (128 if w else -1) + t
                    lane = {-2: 4 * r, -1: 4 * r + 1, 128: 4 * r + 2, 129: 4 * r + 3, 0: 48 + 2 * r, 127: 49 + 2 * r}[col]
                    taps.append((lane, at + OG0 + 2 * (i + 1) + w))
    ocean = [one_hot((128, 128), [(OC0 + 2 * r + j, 4 * r + 2 * e + j) for r in range(12) for j in (0, 1)]) for e in (0, 1)]
    return np.stack([west, east]), one_hot((1664, 128), gather), one_hot((128, 9 * 128), taps), np.stack(ocean)


def grad_side_tables():
    west = one_hot((128, 128 * 10), [(OG0 + 2 * r, 128 * r) for r in range(10)])
    east = one_hot((128, 128 * 10), [(OG0 + 2 * r + 1, 128 * r + 127) for r in range(10)])
    return np.stack([west, east])


def dot(a, b):
    return jnp.dot(a, b, preferred_element_type=F32)


def dot_last(a, b):
    return lax.dot_general(a, b, (((1,), (1,)), ((), ())), preferred_element_type=F32)


def call(kernel, outs, in_specs, scratch=(), limit=32):
    return pl.pallas_call(
        kernel,
        out_shape=[jax.ShapeDtypeStruct(shape, dtype) for shape, dtype in outs],
        in_specs=list(in_specs),
        out_specs=[VMEM] * len(outs),
        scratch_shapes=list(scratch),
        compiler_params=pltpu.CompilerParams(vmem_limit_bytes=limit << 20),
    )


def parcels_kernel(place, sends, ocean, atm, grad, *outs):
    tile = place[0]
    facing = 1 - 2 * (tile & 1)

    def parcel(out, at, shift):
        target = (tile + HALF + shift) & (TILES - 1)
        for slot in range(3):
            block = sends[slot, target]
            start = pl.multiple_of(jnp.maximum(block, 0) * LANES, LANES)
            data = ocean[:, pl.ds(start, LANES)]
            rows = pl.ds(at + 32 * slot, 32)
            out[rows, :] = jnp.where(block >= 0, data, jnp.zeros_like(data))

    for step, out in zip(CHIP_STEPS, outs[:3]):
        parcel(out, 0, 2 * step)
        parcel(out, 96, 2 * step + facing)
    parcel(outs[3], 0, -3 * facing)
    for chan in range(4):
        outs[4][chan, 0:64] = atm[...]
        outs[4][chan, 64:128] = grad[...]


def regrid_kernel(place, sources, blocks, a0, a1, a2, crossed, far, weights, atm, grad, picks, regridded, north, south, sides, held, acc):
    tile = place[0]
    facing = 1 - 2 * (tile & 1)
    for i, ref in enumerate((a0, a1, a2)):
        held[pl.ds(96 * i, 96), :] = ref[0:96, :]
    held[288:576, :] = crossed[0:288, :]
    held[576:672, :] = far[...]
    acc[...] = jnp.zeros_like(acc)
    for k in range(4):
        shift = ((sources[0, k] - tile - HALF + 3 + 2 * TILES) & (TILES - 1)) - 3
        odd = shift & 1
        even_at = 1 - (shift >> 1)
        odd_at = jnp.where(shift == -3 * facing, 6, 4 + ((facing - shift) >> 1))
        at = jnp.clip(jnp.where(odd == 1, odd_at, even_at), 0, 6)
        for slot in range(3):
            block = blocks[0, 3 * k + slot]

            @pl.when(block >= 0)
            def _():
                rows = pl.ds(pl.multiple_of(at * 96 + 32 * slot, 32), 32)
                into = pl.ds(pl.multiple_of(block * 32, 32), 32)
                acc[into, :] += dot(held[rows, :], weights[3 * k + slot])

    for a in range(8):
        regridded[:, LANES * a : LANES * (a + 1)] = acc[32 * a : 32 * (a + 1), :].astype(BF)
    north[:, 0:256] = atm[:, 0:256]
    north[:, 256:384] = grad[:, 0:128]
    north[0:32, 384:512] = regridded[:, 0:128]
    north[32:64, 384:512] = regridded[:, 128:256]
    south[:, 0:256] = atm[:, 768:1024]
    south[:, 256:384] = grad[:, 896:1024]
    south[0:32, 384:512] = regridded[:, 768:896]
    south[32:64, 384:512] = regridded[:, 896:1024]
    edges = dot(atm[...], picks[0]) + dot(grad[...], picks[1])
    sides[0:32, :] = (edges[0:32] + dot(regridded[...], picks[2])).astype(BF)
    sides[32:64, :] = edges[32:64].astype(BF)


def select_kernel(place, own_near, mate_near, gathered, corners, beside, own, mate):
    core = place[0] & 1
    for near, out in ((own_near, own), (mate_near, mate)):

        def pick(direction):
            device = near[0, direction]
            here = (device >= 0) & ((device & 1) == core)
            chip = (device & 7) >> 1
            return jnp.where(here, chip, 0), here

        def strip(direction, lanes):
            chip, here = pick(direction)
            data = gathered[chip, :, lanes[0] : lanes[1]]
            return jnp.where(here, data, jnp.zeros_like(data))

        out[:, 0:512] = strip(0, (0, 512))
        out[:, 512:1024] = strip(1, (512, 1024))
        total = jnp.zeros((64, 128), F32)
        halves = [jnp.zeros((32, 128), F32), jnp.zeros((32, 128), F32)]
        for east in (0, 1):
            data = strip(2 + east, (1024, 1152))
            total = total + dot(data, beside[east, 0])
            halves[east] = halves[east] + dot(data[0:32], beside[east, 1])
            for at_south in (0, 1):
                corner = 2 * at_south + east
                data = strip(4 + corner, (512, 1024) if at_south else (0, 512))
                total = total + dot(data, corners[corner, 0])
                halves[east] = halves[east] + dot(data[0:32], corners[corner, 1])
                halves[east] = halves[east] + dot(data[32:64], corners[corner, 2])
        out[0:32, 1024:1152] = (total[0:32] + halves[0]).astype(BF)
        out[32:64, 1024:1152] = (total[32:64] + halves[1]).astype(BF)


def pack_kernel(own, crossed, regridded, bias, shard):
    shard[:, 0:1024] = own[:, 0:1024] + crossed[:, 0:1024]
    side = own[:, 1024:1152].astype(F32) + crossed[:, 1024:1152].astype(F32)
    lane = lax.broadcasted_iota(jnp.int32, (64, 128), 1)
    rest = bias[...]
    for i in range(3):
        part = rest.astype(BF).astype(F32)
        side = jnp.where(lane == BIAS0 + i, part, side)
        rest = rest - part
    shard[:, 1024:1152] = side.astype(BF)
    shard[0:32, 1152:1664] = regridded[:, 0:512]
    shard[32:64, 1152:1664] = regridded[:, 512:1024]


def forward_kernel(
    place, inner, outer, weights, shifts, in_edges, in_gather, in_taps, ocean_sides,
    output, z_all, mine, theirs, plain, taps, side_taps, grads, outs,
):
    chan, core = place[1], place[0] & 1
    for c in range(4):
        atm = slice(64 * c, 64 * c + 64)
        sea = slice(256 + 32 * c, 288 + 32 * c)
        plain[atm, 0:256] = outer[c, :, 0:256]
        plain[atm, 256:1280] = inner[c, 0:64, :]
        plain[atm, 1280:1536] = outer[c, :, 512:768]
        plain[atm, 1536:1664] = outer[c, :, 1024:1152]
        plain[sea, 0:128] = outer[c, 0:32, 384:512]
        plain[sea, 128:256] = outer[c, 32:64, 384:512]
        plain[sea, 256:768] = outer[c, 0:32, 1152:1664]
        plain[sea, 768:1280] = outer[c, 32:64, 1152:1664]
        plain[sea, 1280:1408] = outer[c, 0:32, 896:1024]
        plain[sea, 1408:1536] = outer[c, 32:64, 896:1024]
        side = dot(outer[c, 0:32, 1024:1152], ocean_sides[0]) + dot(outer[c, 32:64, 1024:1152], ocean_sides[1])
        plain[sea, 1536:1664] = side.astype(BF)
        grads[atm, 0:128] = outer[c, :, 256:384]
        grads[atm, 128:1152] = inner[c, 64:128, :]
        grads[atm, 1152:1280] = outer[c, :, 768:896]
        lane = lax.broadcasted_iota(jnp.int32, (64, 128), 1)
        side = outer[c, :, 1024:1152]
        grads[atm, 1280:1408] = jnp.where((lane >= OG0) & (lane < OC0), side, jnp.zeros_like(side))
    side = plain[:, 1536:1664]
    for at, t in ((0, 0), (2, 1)):
        rows = slice(384 * at, 384 * at + 384)
        edges = dot(side, in_edges[t])
        for r in range(12):
            lanes = slice(128 * r, 128 * r + 128)
            moved = dot(plain[:, lanes], shifts[t])
            taps[rows, lanes] = (moved + edges[:, lanes]).astype(BF)
    taps[384:768, :] = plain[:, 0:1536]
    columns = dot(plain[...], in_gather[...]).astype(BF)
    for s in range(3):
        for t in range(3):
            lanes = slice(128 * (3 * s + t), 128 * (3 * s + t) + 128)
            side_taps[384 * t : 384 * t + 384, 128 * s : 128 * s + 128] = dot(columns, in_taps[:, lanes]).astype(BF)
    bias = jnp.concatenate(
        [jnp.sum(outer[c, :, 1024 + BIAS0 : 1024 + BIAS0 + 3].astype(F32), axis=1, keepdims=True) for c in range(4)], axis=0
    )

    def activate(total, lanes):
        pre = total + bias
        gate = 1.0 / (1.0 + jnp.exp(-pre))
        z_all[:, lanes] = (grads[:, lanes].astype(F32) * gate * (1.0 + pre * (1.0 - gate))).astype(BF)
        return pre * gate

    for r in range(0, 10, 2):
        total = jnp.zeros((256, 256), F32)
        for s in range(3):
            total = total + dot(weights[s], taps[:, 128 * (r + s) : 128 * (r + s) + 256])
        silu = activate(total, slice(128 * r, 128 * r + 256))
        for q in (0, 1):
            row = r + q - 1
            if 0 <= row < 8:
                state = plain[0:256, 128 * (row + 2) : 128 * (row + 3)].astype(F32)
                outs[:, 128 * row : 128 * row + 128] = (state + silu[:, 128 * q : 128 * q + 128]).astype(BF)
    total = jnp.zeros((256, 128), F32)
    for s in range(3):
        total = total + dot(weights[s], side_taps[:, 128 * s : 128 * s + 128])
    activate(total, slice(1280, 1408))
    rows = pl.ds(pl.multiple_of(chan * 64, 64), 64)
    output[...] = outs[rows, :]
    own = z_all[rows, 128:1152]
    sums = dot_last(jnp.ones((16, 1024), BF), own)
    for half, first in ((0, mine), (1, theirs)):
        first[54:64] = jnp.zeros((10, 16, 128), F32)
        first[54, :, 0:64] = sums
    for s in range(3):
        found = dot_last(own, taps[:, 128 * (s + 1) : 128 * (s + 1) + 1024])
        for t in range(3):
            for a in range(4):
                for l in range(3):
                    piece = found[16 * a : 16 * a + 16, 384 * t + 128 * l : 384 * t + 128 * l + 128]
                    row = 4 * (3 * s + t) + a
                    half, at = row // 18, (row % 18) * 3 + l

                    @pl.when(core == half)
                    def _():
                        mine[at] = piece

                    @pl.when(core != half)
                    def _():
                        theirs[at] = piece


def backward_kernel(
    place, sources, blocks, z_all, weights, shifts, z_edges, regrid_weights, grad,
    input_grad, r0, r1, r2, far, taps, delta, terms,
):
    tile, chan = place[0], place[1]
    facing = 1 - 2 * (tile & 1)
    side = z_all[:, 1280:1408]
    for at, t in ((0, 1), (2, 0)):
        rows = slice(256 * at, 256 * at + 256)
        edges = dot(side, z_edges[t])
        for r in range(10):
            lanes = slice(128 * r, 128 * r + 128)
            moved = dot(z_all[:, lanes], shifts[t])
            taps[rows, lanes] = (moved + edges[:, lanes]).astype(BF)
    taps[256:512, :] = z_all[:, 0:1280]
    atm_rows = pl.ds(pl.multiple_of(chan * 64, 64), 64)
    sea_rows = pl.ds(pl.multiple_of(256 + chan * 32, 32), 32)
    for q in range(4):
        atm_total = jnp.zeros((64, 256), F32)
        sea_total = jnp.zeros((32, 256), F32)
        for s in range(3):
            first = 128 * (2 * q + 2 - s)
            for t in range(3):
                window = taps[256 * t : 256 * t + 256, first : first + 256]
                atm_total = atm_total + dot(weights[3 * s + t, atm_rows, :], window)
                sea_total = sea_total + dot(weights[3 * s + t, sea_rows, :], window)
        lanes = slice(256 * q, 256 * q + 256)
        input_grad[:, lanes] = (grad[:, lanes].astype(F32) + atm_total).astype(BF)
        delta[:, lanes] = sea_total.astype(BF)
    for e in range(12):
        block = blocks[0, e]
        lanes = pl.ds(pl.multiple_of(jnp.maximum(block, 0) * LANES, LANES), LANES)
        term = dot_last(delta[:, lanes], regrid_weights[e])
        terms[32 * e : 32 * e + 32, :] = jnp.where(block >= 0, term, 0.0).astype(BF)
    terms[384:480, :] = jnp.zeros((96, 128), BF)

    def parcel(out, at, shift):
        target = (tile + HALF + shift) & (TILES - 1)
        found = jnp.int32(4)
        for k in range(4):
            found = jnp.where(sources[0, k] == target, k, found)
        out[at : at + 96, :] = terms[pl.ds(pl.multiple_of(found * 96, 96), 96), :]

    for step, out in zip(CHIP_STEPS, (r0, r1, r2)):
        parcel(out, 0, 2 * step)
        parcel(out, 96, 2 * step + facing)
    parcel(far, 0, -3 * facing)


def return_kernel(place, sends, a0, a1, a2, crossed, far, ocean_grad, acc):
    tile = place[0]
    facing = 1 - 2 * (tile & 1)
    acc[...] = jnp.zeros_like(acc)

    def add(ref, first, shift):
        sender = (tile + HALF + shift) & (TILES - 1)
        for slot in range(3):
            block = sends[slot, sender]

            @pl.when(block >= 0)
            def _():
                into = pl.ds(pl.multiple_of(block * 32, 32), 32)
                acc[into, :] += ref[first + 32 * slot : first + 32 * slot + 32, :].astype(F32)

    for i, (step, ref) in enumerate(zip(CHIP_STEPS, (a0, a1, a2))):
        add(ref, 0, -2 * step)
        add(crossed, 96 * i, -2 * step + facing)
    add(far, 0, -3 * facing)
    for b in range(8):
        ocean_grad[:, LANES * b : LANES * (b + 1)] = acc[32 * b : 32 * (b + 1), :]


def sum_kernel(scale, arrived, out):
    total = jnp.sum(arrived[...].astype(F32), axis=0) * scale
    for i in range(64):
        out[i] = total.astype(BF)


def finish_kernel(place, held, crossed, weight_grad, bias_grad):
    core = place[0] & 1
    for half in range(2):
        for a in range(18):
            row = 18 * half + a
            k, part = row // 4, row % 4
            for l in range(3):
                at = 3 * a + l
                piece = jnp.where(core == half, held[at].astype(F32), crossed[at].astype(F32))
                weight_grad[k, 16 * part : 16 * part + 16, 128 * l : 128 * l + 128] = piece
    bias_grad[...] = held[54].astype(F32)[0:8]


def send(array, target):
    return lax.ppermute(array, "tile", [(i, target(i)) for i in range(TILES)])


def spread(a0, a1, a2, far):
    moved = [send(a, lambda i, step=step: (i + HALF + 2 * step) % TILES) for step, a in zip(CHIP_STEPS, (a0, a1, a2))]
    beyond = send(far, lambda i: (i + HALF - 3 * (1 - 2 * (i % 2))) % TILES)
    return moved, beyond


def to_mate(array):
    return send(array, lambda i: i ^ 1)


def on_device(
    atm_state,
    ocean_state,
    conv_weight,
    conv_bias,
    regrid_weight,
    out_grad,
    atm_neighbours,
    coupling_sources,
    coupling_blocks,
    coupling_sends,
):
    place = jnp.stack([lax.axis_index("tile"), lax.axis_index("chan")]).astype(jnp.int32)
    sends = coupling_sends[0].T
    flipped = jnp.swapaxes(conv_weight.reshape(3, 1152, 256), 1, 2)
    b0, b1, b2, far, copies = call(
        parcels_kernel, [((192, 128), BF)] * 3 + [((96, 128), BF), ((4, 128, 1024), BF)], [SMEM, SMEM, VMEM, VMEM, VMEM]
    )(place, sends, ocean_state, atm_state, out_grad)
    inner = lax.all_to_all(copies, "chan", 0, 0)
    (a0, a1, a2), far = spread(b0, b1, b2, far)
    table = jnp.pad(atm_neighbours.astype(BF), ((0, 15), (0, 120)))
    crossed = to_mate(jnp.concatenate([a0[96:], a1[96:], a2[96:], table], axis=0))
    mate_near = crossed[288:289, 0:8].astype(jnp.int32)
    regridded, north, south, sides = call(
        regrid_kernel,
        [((32, 1024), BF), ((64, 512), BF), ((64, 512), BF), ((64, 128), BF)],
        [SMEM] * 3 + [VMEM] * 9,
        [pltpu.VMEM((672, 128), BF), pltpu.VMEM((256, 128), F32)],
    )(place, coupling_sources, coupling_blocks, a0, a1, a2, crossed, far, regrid_weight, atm_state, out_grad, jnp.asarray(edge_tables()))
    from_north = lax.ppermute(south, "tile", [(i, i + 8) for i in range(TILES - 8)])
    from_south = lax.ppermute(north, "tile", [(i + 8, i) for i in range(TILES - 8)])
    strips = lax.all_gather(jnp.concatenate([from_north, from_south, sides], axis=1), "tile", axis_index_groups=ROW_CHIPS)
    own, mate = call(select_kernel, [((64, 1152), BF)] * 2, [SMEM] * 3 + [VMEM] * 3)(
        place, atm_neighbours, mate_near, strips, jnp.asarray(corner_tables()), jnp.asarray(beside_tables())
    )
    crossed = to_mate(mate)
    (shard,) = call(pack_kernel, [((64, 1664), BF)], [VMEM] * 4)(own, crossed, regridded, conv_bias.reshape(64, 1))
    outer = lax.all_gather(shard, "chan")
    in_edges, in_gather, in_taps, ocean_sides = (jnp.asarray(table) for table in input_side_tables())
    shifts = jnp.asarray(shift_tables())
    atm_output, z_all, mine, theirs = call(
        forward_kernel,
        [((64, 1024), BF), ((256, 1408), BF), ((64, 16, 128), F32), ((64, 16, 128), F32)],
        [SMEM] + [VMEM] * 8,
        [
            pltpu.VMEM((384, 1664), BF),
            pltpu.VMEM((1152, 1536), BF),
            pltpu.VMEM((1152, 384), BF),
            pltpu.VMEM((256, 1408), BF),
            pltpu.VMEM((256, 1024), BF),
        ],
        limit=48,
    )(place, inner, outer, flipped, shifts, in_edges, in_gather, in_taps, ocean_sides)
    theirs = to_mate(theirs)
    input_grad, b0, b1, b2, far = call(
        backward_kernel,
        [((64, 1024), BF)] + [((192, 128), BF)] * 3 + [((96, 128), BF)],
        [SMEM] * 3 + [VMEM] * 6,
        [pltpu.VMEM((768, 1280), BF), pltpu.VMEM((32, 1024), BF), pltpu.VMEM((480, 128), BF)],
        limit=48,
    )(place, coupling_sources, coupling_blocks, z_all, conv_weight, shifts, jnp.asarray(grad_side_tables()), regrid_weight, out_grad)
    shares = lax.all_to_all((mine + theirs).astype(BF), "tile", 0, 0, axis_index_groups=SAME_CORE)
    (a0, a1, a2), far = spread(b0, b1, b2, far)
    crossed = to_mate(jnp.concatenate([a0[96:], a1[96:], a2[96:]], axis=0))
    (ocean_grad,) = call(return_kernel, [((32, 1024), F32)], [SMEM] * 2 + [VMEM] * 5, [pltpu.VMEM((256, 128), F32)])(
        place, sends, a0, a1, a2, crossed, far
    )
    scale = 1.0 / math.sqrt(atm_state.shape[1] * TILES)
    (summed,) = call(functools.partial(sum_kernel, scale), [((64, 16, 128), BF)], [VMEM])(shares)
    held = lax.all_to_all(summed, "tile", 0, 0, axis_index_groups=SAME_CORE)
    crossed = to_mate(held)
    weight_grad, bias_grad = call(finish_kernel, [((9, 64, 384), F32), ((8, 128), F32)], [SMEM, VMEM, VMEM])(place, held, crossed)
    return atm_output, input_grad, ocean_grad, jnp.swapaxes(weight_grad, 1, 2), bias_grad[0, 0:64]


def solution(mesh):
    placed = (
        P("chan", "tile"),
        P("chan", "tile"),
        P(),
        P("chan"),
        P("tile", None, None),
        P("chan", "tile"),
        P("tile", None),
        P("tile", None),
        P("tile", None),
        P("tile", None, None),
    )
    return jax.shard_map(
        on_device,
        mesh=mesh,
        in_specs=placed,
        out_specs=(
            P("chan", "tile"),
            P("chan", "tile"),
            P("chan", "tile"),
            P(None, None, "chan"),
            P("chan"),
        ),
        check_vma=False,
    )
```

```python
import functools
import math

import jax
import jax.numpy as jnp
from jax import lax
from jax.experimental import pallas as pl
from jax.experimental.pallas import tpu as pltpu
from jax.sharding import PartitionSpec as P

BF, F32 = jnp.bfloat16, jnp.float32
TILES = 128
HALF = TILES // 2
LANES = 128
OG0, OC0, BIAS0 = 48, 68, 92
VMEM = pl.BlockSpec(memory_space=pltpu.VMEM)
SMEM = pl.BlockSpec(memory_space=pltpu.SMEM)
HELD = pl.BlockSpec(memory_space=pl.ANY)

CHIP_STEPS = (-1, 0, 1)
ROW_CHIPS = [[8 * r + 2 * i + c for i in range(4)] for r in range(16) for c in range(2)]
SAME_CORE = [[2 * i + c for i in range(64)] for c in range(2)]


def grid(rows, columns):
    shape = (rows, columns)
    return lax.broadcasted_iota(jnp.int32, shape, 0), lax.broadcasted_iota(jnp.int32, shape, 1)


def marks(where):
    return jnp.where(where, 1.0, 0.0).astype(BF)


def edge_table(first):
    cell, lane = grid(1024, 128)
    col, at = cell & 127, first + 2 * (cell >> 7)
    return marks(((col < 2) & (lane == at + col)) | ((col >= 126) & (lane == at + col - 110)))


def grad_edge_table():
    cell, lane = grid(1024, 128)
    col, row = cell & 127, cell >> 7
    return marks(((col == 0) & (lane == 32 + row)) | ((col == 127) & (lane == 40 + row)))


def pair_table(given, to):
    lane, into = grid(128, 128)
    return marks((lane >= given) & (lane < given + 2) & (into - to == lane - given))


def single_table(given, to):
    lane, into = grid(128, 128)
    return marks((lane == given) & (into == to))


def beside_table(given, to, step):
    lane, into = grid(128, 128)
    at = lane - given
    return marks((at >= 0) & (at < 16) & (into == to + step * (at >> 1) + (at & 1)))


def beside_grad_table(given, to):
    lane, into = grid(128, 128)
    at = lane - given
    return marks((at >= 0) & (at < 8) & (into == to + 2 * at))


def shift_table(step):
    lane, into = grid(128, 128)
    return marks(lane == into + step)


def shift_tables():
    return jnp.concatenate([shift_table(-1), shift_table(1)], axis=1)


def edge_rows():
    lane, into = grid(128, 256)
    return jnp.where(into == 0, lane, jnp.where(into == 255, lane - 1, -8))


def edge_marks(rows, first):
    return marks(rows == first)


def gather_table():
    lane, into = grid(1536, 128)
    col, row = lane & 127, lane >> 7
    return marks(((col == 0) & (into == 48 + 2 * row)) | ((col == 127) & (into == 49 + 2 * row)))


def tap_table(s, t):
    lane, into = grid(128, 128)
    at = into - OG0
    east, row = at & 1, (at >> 1) + s + 1
    col = jnp.where(east == 1, 128, -1) + t
    near = jnp.where(col == 0, 48 + 2 * row, 49 + 2 * row)
    far = jnp.where(col < 0, 4 * row + col + 2, 4 * row + col - 126)
    given = jnp.where((col == 0) | (col == 127), near, far)
    return marks((at >= 0) & (at < 20) & (lane == given))


def ocean_side_table(east):
    lane, into = grid(128, 128)
    at = lane - OC0
    return marks((at >= 0) & (at < 24) & (into == 4 * (at >> 1) + (at & 1) + 2 * east))


def dot(a, b):
    return jnp.dot(a, b, preferred_element_type=F32)


def dot_last(a, b):
    return lax.dot_general(a, b, (((1,), (1,)), ((), ())), preferred_element_type=F32)


def call(kernel, outs, in_specs, scratch=(), limit=32, cost=1):
    return pl.pallas_call(
        kernel,
        out_shape=[jax.ShapeDtypeStruct(shape, dtype) for shape, dtype in outs],
        in_specs=list(in_specs),
        out_specs=[VMEM] * len(outs),
        scratch_shapes=list(scratch),
        compiler_params=pltpu.CompilerParams(vmem_limit_bytes=limit << 20),
        cost_estimate=pl.CostEstimate(flops=cost * 10**9, bytes_accessed=cost * 3 * 10**6, transcendentals=0),
    )


def parcels_kernel(sends, ocean, *outs):
    tile = lax.axis_index("tile")
    facing = 1 - 2 * (tile & 1)

    def parcel(out, at, shift):
        target = (tile + HALF + shift) & (TILES - 1)
        for slot in range(3):
            block = sends[slot, target]
            start = pl.multiple_of(jnp.maximum(block, 0) * LANES, LANES)
            data = ocean[:, pl.ds(start, LANES)]
            rows = pl.ds(at + 32 * slot, 32)
            out[rows, :] = jnp.where(block >= 0, data, jnp.zeros_like(data))

    for step, out in zip(CHIP_STEPS, outs[:3]):
        parcel(out, 0, 2 * step)
        parcel(out, 96, 2 * step + facing)
    parcel(outs[3], 0, -3 * facing)


def copies_kernel(atm, grad, copies):
    for chan in range(4):
        copies[chan, 0:64] = atm[...]
        copies[chan, 64:128] = grad[...]


def regrid_kernel(sources, blocks, a0, a1, a2, crossed, far, weights, atm, grad, regridded, north, south, sides, held, acc):
    tile = lax.axis_index("tile")
    facing = 1 - 2 * (tile & 1)
    for i, ref in enumerate((a0, a1, a2)):
        held[pl.ds(96 * i, 96), :] = ref[0:96, :]
    held[288:576, :] = crossed[0:288, :]
    held[576:672, :] = far[...]
    acc[...] = jnp.zeros_like(acc)
    for k in range(4):
        shift = ((sources[0, k] - tile - HALF + 3 + 2 * TILES) & (TILES - 1)) - 3
        odd = shift & 1
        even_at = 1 - (shift >> 1)
        odd_at = jnp.where(shift == -3 * facing, 6, 4 + ((facing - shift) >> 1))
        at = jnp.clip(jnp.where(odd == 1, odd_at, even_at), 0, 6)
        for slot in range(3):
            block = blocks[0, 3 * k + slot]

            @pl.when(block >= 0)
            def _():
                rows = pl.ds(pl.multiple_of(at * 96 + 32 * slot, 32), 32)
                into = pl.ds(pl.multiple_of(block * 32, 32), 32)
                acc[into, :] += dot(held[rows, :], weights[3 * k + slot])

    for a in range(8):
        regridded[:, LANES * a : LANES * (a + 1)] = acc[32 * a : 32 * (a + 1), :].astype(BF)
    north[:, 0:256] = atm[:, 0:256]
    north[:, 256:384] = grad[:, 0:128]
    north[0:32, 384:512] = regridded[:, 0:128]
    north[32:64, 384:512] = regridded[:, 128:256]
    south[:, 0:256] = atm[:, 768:1024]
    south[:, 256:384] = grad[:, 896:1024]
    south[0:32, 384:512] = regridded[:, 768:896]
    south[32:64, 384:512] = regridded[:, 896:1024]
    edges = dot(atm[...], edge_table(0)) + dot(grad[...], grad_edge_table())
    sides[0:32, :] = (edges[0:32] + dot(regridded[...], edge_table(64))).astype(BF)
    sides[32:64, :] = edges[32:64].astype(BF)


def select_kernel(own_near, mate_near, gathered, regridded, bias, own, mate):
    core = lax.axis_index("tile") & 1
    for near, out in ((own_near, own), (mate_near, mate)):

        def pick(direction):
            device = near[0, direction]
            here = (device >= 0) & ((device & 1) == core)
            chip = (device & 7) >> 1
            return jnp.where(here, chip, 0), here

        def strip(direction, lanes):
            chip, here = pick(direction)
            data = gathered[chip, :, lanes[0] : lanes[1]]
            return jnp.where(here, data, jnp.zeros_like(data))

        out[:, 0:512] = strip(0, (0, 512))
        out[:, 512:1024] = strip(1, (512, 1024))
        total = jnp.zeros((64, 128), F32)
        halves = [jnp.zeros((32, 128), F32), jnp.zeros((32, 128), F32)]
        for east in (0, 1):
            data = strip(2 + east, (1024, 1152))
            given = 0 if east else 16
            picks = beside_table(given, 8 + 2 * east, 4) + beside_grad_table(32 if east else 40, OG0 + 2 + east)
            total = total + dot(data, picks)
            halves[east] = halves[east] + dot(data[0:32], beside_table(64 + given, OC0 + 4, 2))
            col = 0 if east else 126
            for at_south in (0, 1):
                first, beyond = (10, 9) if at_south else (0, 0)
                data = strip(4 + 2 * at_south + east, (512, 1024) if at_south else (0, 512))
                for q in (0, 1):
                    total = total + dot(data[:, 128 * q : 128 * q + 128], pair_table(col, 4 * (first + q) + 2 * east))
                    halves[east] = halves[east] + dot(data[32 * q : 32 * q + 32, 384:512], pair_table(col, OC0 + 2 * (first + q)))
                total = total + dot(data[:, 256:384], single_table(0 if east else 127, OG0 + 2 * beyond + east))
        out[0:32, 1024:1152] = (total[0:32] + halves[0]).astype(BF)
        out[32:64, 1024:1152] = (total[32:64] + halves[1]).astype(BF)
    side = own[:, 1024:1152].astype(F32)
    row, _ = grid(64, 64)
    _, lane = grid(64, 128)
    rest = jnp.sum(jnp.where(row == lane[:, 0:64], bias[...], 0.0), axis=1, keepdims=True)
    for i in range(3):
        part = rest.astype(BF).astype(F32)
        side = jnp.where(lane == BIAS0 + i, part, side)
        rest = rest - part
    own[:, 1024:1152] = side.astype(BF)
    own[0:32, 1152:1664] = regridded[:, 0:512]
    own[32:64, 1152:1664] = regridded[:, 512:1024]


def forward_kernel(
    inner, outer_held, flipped, output, z_all, mine, theirs, side_atm, taps, side_taps, grads, outs, weights, outer, lifted, sems
):
    chan, core = lax.axis_index("chan"), lax.axis_index("tile") & 1
    fetches = [pltpu.make_async_copy(outer_held, outer, sems.at[0])]
    for c in range(4):
        own = slice(64 * c, 64 * c + 64)
        state = taps.at[pl.ds(384 + 64 * c, 64), pl.ds(256, 1024)]
        fetches.append(pltpu.make_async_copy(inner.at[c, pl.ds(0, 64)], state, sems.at[1 + c]))
        fetches.append(pltpu.make_async_copy(inner.at[c, pl.ds(64, 64)], grads.at[own, pl.ds(128, 1024)], sems.at[5 + c]))
    fetches.append(pltpu.make_async_copy(flipped, weights, sems.at[9]))
    for fetch in fetches:
        fetch.start()
    fetches[0].wait()
    _, lane = grid(64, 128)
    for c in range(4):
        atm = slice(64 * c, 64 * c + 64)
        mid = slice(384 + 64 * c, 448 + 64 * c)
        sea = slice(640 + 32 * c, 672 + 32 * c)
        taps[mid, 0:256] = outer[c, :, 0:256]
        taps[mid, 1280:1536] = outer[c, :, 512:768]
        side_atm[atm, :] = outer[c, :, 1024:1152]
        taps[sea, 0:128] = outer[c, 0:32, 384:512]
        taps[sea, 128:256] = outer[c, 32:64, 384:512]
        taps[sea, 256:768] = outer[c, 0:32, 1152:1664]
        taps[sea, 768:1280] = outer[c, 32:64, 1152:1664]
        taps[sea, 1280:1408] = outer[c, 0:32, 896:1024]
        taps[sea, 1408:1536] = outer[c, 32:64, 896:1024]
        side = dot(outer[c, 0:32, 1024:1152], ocean_side_table(0)) + dot(outer[c, 32:64, 1024:1152], ocean_side_table(1))
        side_atm[256 + 32 * c : 288 + 32 * c, :] = side.astype(BF)
        grads[atm, 0:128] = outer[c, :, 256:384]
        grads[atm, 1152:1280] = outer[c, :, 768:896]
        side = outer[c, :, 1024:1152]
        grads[atm, 1280:1408] = jnp.where((lane >= OG0) & (lane < OC0), side, jnp.zeros_like(side))
    for fetch in fetches[1:9]:
        fetch.wait()
    side = side_atm[...]
    shifts, edges = shift_tables(), edge_rows()
    for r in range(12):
        lanes = slice(128 * r, 128 * r + 128)
        table = jnp.concatenate([shifts, edge_marks(edges, 4 * r + 1)], axis=0)
        moved = dot(jnp.concatenate([taps[384:768, lanes], side], axis=1), table).astype(BF)
        taps[0:384, lanes] = moved[:, 0:128]
        taps[768:1152, lanes] = moved[:, 128:256]
    _, lane = grid(384, 128)
    columns = dot(taps[384:768, :], gather_table()).astype(BF)
    columns = jnp.where(lane < 48, side, columns)
    moved = dot(columns, jnp.concatenate([tap_table(s, t) for s in (-1, 0, 1) for t in (-1, 0, 1)], axis=1)).astype(BF)
    for s in range(3):
        for t in range(3):
            at = 128 * (3 * s + t)
            side_taps[384 * t : 384 * t + 384, 128 * s : 128 * s + 128] = moved[:, at : at + 128]
    bias = jnp.concatenate(
        [jnp.sum(outer[c, :, 1024 + BIAS0 : 1024 + BIAS0 + 3].astype(F32), axis=1, keepdims=True) for c in range(4)], axis=0
    )

    fetches[9].wait()

    def activate(total, lanes):
        pre = total + bias
        gate = 1.0 / (1.0 + jnp.exp(-pre))
        z_all[:, lanes] = (grads[:, lanes].astype(F32) * gate * (1.0 + pre * (1.0 - gate))).astype(BF)
        return pre * gate

    for r in range(0, 10, 2):
        total = jnp.zeros((256, 256), F32)
        for s in range(3):
            total = total + dot(weights[s], taps[:, 128 * (r + s) : 128 * (r + s) + 256])
        silu = activate(total, slice(128 * r, 128 * r + 256))
        for q in (0, 1):
            row = r + q - 1
            if 0 <= row < 8:
                state = taps[384:640, 128 * (row + 2) : 128 * (row + 3)].astype(F32)
                outs[:, 128 * row : 128 * row + 128] = (state + silu[:, 128 * q : 128 * q + 128]).astype(BF)
    total = jnp.zeros((256, 128), F32)
    for s in range(3):
        total = total + dot(weights[s], side_taps[:, 128 * s : 128 * s + 128])
    activate(total, slice(1280, 1408))
    rows = pl.ds(pl.multiple_of(chan * 64, 64), 64)
    output[...] = outs[rows, :]
    own = z_all[rows, 128:1152]
    sums = dot_last(jnp.ones((16, 1024), BF), own)
    for half, first in ((0, mine), (1, theirs)):
        first[54:64] = jnp.zeros((10, 16, 128), F32)
        first[54, :, 0:64] = sums
    lifted[...] = jnp.zeros_like(lifted)
    for s in range(3):
        lifted[64 * s : 64 * s + 64, 128 * (s + 1) : 128 * (s + 1) + 1024] = own
    found = dot_last(lifted[...], taps[...])
    for s in range(3):
        for t in range(3):
            for a in range(4):
                for l in range(3):
                    piece = found[64 * s + 16 * a : 64 * s + 16 * a + 16, 384 * t + 128 * l : 384 * t + 128 * l + 128]
                    row = 4 * (3 * s + t) + a
                    half, at = row // 18, (row % 18) * 3 + l

                    @pl.when(core == half)
                    def _():
                        mine[at] = piece

                    @pl.when(core != half)
                    def _():
                        theirs[at] = piece


def backward_kernel(
    sources, blocks, z_all, weights_held, regrid_weights, grad,
    input_grad, r0, r1, r2, far, taps, delta, terms, weights, sem,
):
    fetch = pltpu.make_async_copy(weights_held, weights, sem)
    fetch.start()
    tile, chan = lax.axis_index("tile"), lax.axis_index("chan")
    facing = 1 - 2 * (tile & 1)
    side = z_all[:, 1280:1408]
    shifts, edges = shift_tables(), edge_rows()
    for r in range(10):
        lanes = slice(128 * r, 128 * r + 128)
        table = jnp.concatenate([shifts, edge_marks(edges, OG0 + 2 * r)], axis=0)
        moved = dot(jnp.concatenate([z_all[:, lanes], side], axis=1), table).astype(BF)
        taps[512:768, lanes] = moved[:, 0:128]
        taps[0:256, lanes] = moved[:, 128:256]
    taps[256:512, :] = z_all[:, 0:1280]
    atm_rows = pl.ds(pl.multiple_of(chan * 64, 64), 64)
    sea_rows = pl.ds(pl.multiple_of(256 + chan * 32, 32), 32)
    fetch.wait()
    for q in range(4):
        atm_total = jnp.zeros((64, 256), F32)
        sea_total = jnp.zeros((32, 256), F32)
        for s in range(3):
            first = 128 * (2 * q + 2 - s)
            for t in range(3):
                window = taps[256 * t : 256 * t + 256, first : first + 256]
                atm_total = atm_total + dot(weights[3 * s + t, atm_rows, :], window)
                sea_total = sea_total + dot(weights[3 * s + t, sea_rows, :], window)
        lanes = slice(256 * q, 256 * q + 256)
        input_grad[:, lanes] = (grad[:, lanes].astype(F32) + atm_total).astype(BF)
        delta[:, lanes] = sea_total.astype(BF)
    for e in range(12):
        block = blocks[0, e]
        lanes = pl.ds(pl.multiple_of(jnp.maximum(block, 0) * LANES, LANES), LANES)
        term = dot_last(delta[:, lanes], regrid_weights[e])
        terms[32 * e : 32 * e + 32, :] = jnp.where(block >= 0, term, 0.0).astype(BF)
    terms[384:480, :] = jnp.zeros((96, 128), BF)

    def parcel(out, at, shift):
        target = (tile + HALF + shift) & (TILES - 1)
        found = jnp.int32(4)
        for k in range(4):
            found = jnp.where(sources[0, k] == target, k, found)
        out[at : at + 96, :] = terms[pl.ds(pl.multiple_of(found * 96, 96), 96), :]

    for step, out in zip(CHIP_STEPS, (r0, r1, r2)):
        parcel(out, 0, 2 * step)
        parcel(out, 96, 2 * step + facing)
    parcel(far, 0, -3 * facing)


def return_kernel(sends, a0, a1, a2, crossed, far, ocean_grad, acc):
    tile = lax.axis_index("tile")
    facing = 1 - 2 * (tile & 1)
    acc[...] = jnp.zeros_like(acc)

    def add(ref, first, shift):
        sender = (tile + HALF + shift) & (TILES - 1)
        for slot in range(3):
            block = sends[slot, sender]

            @pl.when(block >= 0)
            def _():
                into = pl.ds(pl.multiple_of(block * 32, 32), 32)
                acc[into, :] += ref[first + 32 * slot : first + 32 * slot + 32, :].astype(F32)

    for i, (step, ref) in enumerate(zip(CHIP_STEPS, (a0, a1, a2))):
        add(ref, 0, -2 * step)
        add(crossed, 96 * i, -2 * step + facing)
    add(far, 0, -3 * facing)
    for b in range(8):
        ocean_grad[:, LANES * b : LANES * (b + 1)] = acc[32 * b : 32 * (b + 1), :]


def sum_kernel(scale, arrived, out):
    total = (jnp.sum(arrived[...].astype(F32), axis=0) * scale).astype(BF)
    for i in range(64):
        out[i] = total


def finish_kernel(held, crossed, weight_grad, bias_grad):
    core = lax.axis_index("tile") & 1
    for half in range(2):
        for a in range(18):
            row = 18 * half + a
            k, part = row // 4, row % 4
            for l in range(3):
                at = 3 * a + l
                piece = jnp.where(core == half, held[at].astype(F32), crossed[at].astype(F32))
                weight_grad[k, 16 * part : 16 * part + 16, 128 * l : 128 * l + 128] = piece
    bias_grad[...] = held[54].astype(F32)[0:8]


def send(array, target):
    return lax.ppermute(array, "tile", [(i, target(i)) for i in range(TILES)])


def chip_send(array, at):
    return send(array, lambda i: (i + HALF + 2 * CHIP_STEPS[at]) % TILES)


def far_send(array):
    return send(array, lambda i: (i + HALF - 3 * (1 - 2 * (i % 2))) % TILES)


def to_mate(array):
    return send(array, lambda i: i ^ 1)


def on_device(
    atm_state,
    ocean_state,
    conv_weight,
    conv_bias,
    regrid_weight,
    out_grad,
    atm_neighbours,
    coupling_sources,
    coupling_blocks,
    coupling_sends,
):
    sends = coupling_sends[0].T
    flipped = jnp.swapaxes(conv_weight.reshape(3, 1152, 256), 1, 2)
    b0, b1, b2, far = call(parcels_kernel, [((192, 128), BF)] * 3 + [((96, 128), BF)], [SMEM, VMEM])(sends, ocean_state)
    (copies,) = call(copies_kernel, [((4, 128, 1024), BF)], [VMEM, VMEM])(atm_state, out_grad)
    inner = lax.all_to_all(copies, "chan", 0, 0)
    a0, a1, a2, far = chip_send(b0, 0), chip_send(b1, 1), chip_send(b2, 2), far_send(far)
    far, flipped = lax.optimization_barrier((far, flipped))
    table = jnp.pad(atm_neighbours.astype(BF), ((0, 15), (0, 120)))
    crossed = to_mate(jnp.concatenate([a0[96:], a1[96:], a2[96:], table], axis=0))
    mate_near = crossed[288:289, 0:8].astype(jnp.int32)
    regridded, north, south, sides = call(
        regrid_kernel,
        [((32, 1024), BF), ((64, 512), BF), ((64, 512), BF), ((64, 128), BF)],
        [SMEM] * 2 + [VMEM] * 8,
        [pltpu.VMEM((672, 128), BF), pltpu.VMEM((256, 128), F32)],
    )(coupling_sources, coupling_blocks, a0, a1, a2, crossed, far, regrid_weight, atm_state, out_grad)
    from_north = lax.ppermute(south, "tile", [(i, i + 8) for i in range(TILES - 8)])
    from_south = lax.ppermute(north, "tile", [(i + 8, i) for i in range(TILES - 8)])
    strips = jnp.concatenate([from_north, from_south, sides], axis=1)
    strips, inner = lax.optimization_barrier((strips, inner))
    strips = lax.all_gather(strips, "tile", axis_index_groups=ROW_CHIPS)
    own, mate = call(select_kernel, [((64, 1664), BF), ((64, 1152), BF)], [SMEM] * 2 + [VMEM] * 3)(
        atm_neighbours, mate_near, strips, regridded, conv_bias.reshape(1, 64)
    )
    shard = own + jnp.pad(to_mate(mate), ((0, 0), (0, 512)))
    outer = lax.all_gather(shard, "chan")
    atm_output, z_all, mine, theirs = call(
        forward_kernel,
        [((64, 1024), BF), ((256, 1408), BF), ((64, 16, 128), F32), ((64, 16, 128), F32)],
        [HELD] * 3,
        [
            pltpu.VMEM((384, 128), BF),
            pltpu.VMEM((1152, 1536), BF),
            pltpu.VMEM((1152, 384), BF),
            pltpu.VMEM((256, 1408), BF),
            pltpu.VMEM((256, 1024), BF),
            pltpu.VMEM((3, 256, 1152), BF),
            pltpu.VMEM((4, 64, 1664), BF),
            pltpu.VMEM((192, 1536), BF),
            pltpu.SemaphoreType.DMA((10,)),
        ],
        limit=60,
        cost=10,
    )(inner, outer, flipped)
    total = (mine + to_mate(theirs)).astype(BF)
    total, z_all = lax.optimization_barrier((total, z_all))
    shares = lax.all_to_all(total, "tile", 0, 0, axis_index_groups=SAME_CORE)
    input_grad, b0, b1, b2, far = call(
        backward_kernel,
        [((64, 1024), BF)] + [((192, 128), BF)] * 3 + [((96, 128), BF)],
        [SMEM] * 2 + [VMEM, HELD, VMEM, VMEM],
        [
            pltpu.VMEM((768, 1280), BF),
            pltpu.VMEM((32, 1024), BF),
            pltpu.VMEM((480, 128), BF),
            pltpu.VMEM((9, 384, 256), BF),
            pltpu.SemaphoreType.DMA,
        ],
        limit=48,
        cost=4,
    )(coupling_sources, coupling_blocks, z_all, conv_weight, regrid_weight, out_grad)
    a0, a1, a2 = chip_send(b0, 0), chip_send(b1, 1), chip_send(b2, 2)
    shares, a0, a1, a2, far = lax.optimization_barrier((shares, a0, a1, a2, far))
    scale = 1.0 / math.sqrt(atm_state.shape[1] * TILES)
    (summed,) = call(functools.partial(sum_kernel, scale), [((64, 16, 128), BF)], [VMEM])(shares)
    summed, far = lax.optimization_barrier((summed, far))
    held = lax.all_to_all(summed, "tile", 0, 0, axis_index_groups=SAME_CORE)
    far = far_send(far)
    crossed = to_mate(jnp.concatenate([a0[96:], a1[96:], a2[96:]], axis=0))
    (ocean_grad,) = call(return_kernel, [((32, 1024), F32)], [SMEM] + [VMEM] * 5, [pltpu.VMEM((256, 128), F32)])(
        sends, a0, a1, a2, crossed, far
    )
    held, ocean_grad = lax.optimization_barrier((held, ocean_grad))
    crossed = to_mate(held)
    weight_grad, bias_grad = call(finish_kernel, [((9, 64, 384), F32), ((8, 128), F32)], [VMEM, VMEM])(held, crossed)
    return atm_output, input_grad, ocean_grad, jnp.swapaxes(weight_grad, 1, 2), bias_grad[0, 0:64]


def solution(mesh):
    placed = (
        P("chan", "tile"),
        P("chan", "tile"),
        P(),
        P("chan"),
        P("tile", None, None),
        P("chan", "tile"),
        P("tile", None),
        P("tile", None),
        P("tile", None),
        P("tile", None, None),
    )
    return jax.shard_map(
        on_device,
        mesh=mesh,
        in_specs=placed,
        out_specs=(
            P("chan", "tile"),
            P("chan", "tile"),
            P("chan", "tile"),
            P(None, None, "chan"),
            P("chan"),
        ),
        check_vma=False,
    )
```

```python
import functools
import math

import jax
import jax.numpy as jnp
from jax import lax
from jax.experimental import pallas as pl
from jax.experimental.pallas import tpu as pltpu
from jax.sharding import PartitionSpec as P

BF, F32 = jnp.bfloat16, jnp.float32
TILES = 128
HALF = TILES // 2
LANES = 128
OG0, OC0, BIAS0 = 48, 68, 92
VMEM = pl.BlockSpec(memory_space=pltpu.VMEM)
SMEM = pl.BlockSpec(memory_space=pltpu.SMEM)
HELD = pl.BlockSpec(memory_space=pl.ANY)

CHIP_STEPS = (-1, 0, 1)
ROW_CHIPS = [[8 * r + 2 * i + c for i in range(4)] for r in range(16) for c in range(2)]
SAME_CORE = [[2 * i + c for i in range(64)] for c in range(2)]


def grid(rows, columns):
    shape = (rows, columns)
    return lax.broadcasted_iota(jnp.int32, shape, 0), lax.broadcasted_iota(jnp.int32, shape, 1)


def marks(where):
    return jnp.where(where, 1.0, 0.0).astype(BF)


def edge_table(first):
    cell, lane = grid(1024, 128)
    col, at = cell & 127, first + 2 * (cell >> 7)
    return marks(((col < 2) & (lane == at + col)) | ((col >= 126) & (lane == at + col - 110)))


def grad_edge_table():
    cell, lane = grid(1024, 128)
    col, row = cell & 127, cell >> 7
    return marks(((col == 0) & (lane == 32 + row)) | ((col == 127) & (lane == 40 + row)))


def pair_table(given, to):
    lane, into = grid(128, 128)
    return marks((lane >= given) & (lane < given + 2) & (into - to == lane - given))


def single_table(given, to):
    lane, into = grid(128, 128)
    return marks((lane == given) & (into == to))


def beside_table(given, to, step):
    lane, into = grid(128, 128)
    at = lane - given
    return marks((at >= 0) & (at < 16) & (into == to + step * (at >> 1) + (at & 1)))


def beside_grad_table(given, to):
    lane, into = grid(128, 128)
    at = lane - given
    return marks((at >= 0) & (at < 8) & (into == to + 2 * at))


def shift_table(step):
    lane, into = grid(128, 128)
    return marks(lane == into + step)


def shift_tables():
    return jnp.concatenate([shift_table(-1), shift_table(1)], axis=1)


def edge_rows():
    lane, into = grid(128, 256)
    return jnp.where(into == 0, lane, jnp.where(into == 255, lane - 1, -8))


def edge_marks(rows, first):
    return marks(rows == first)


def gather_table():
    lane, into = grid(1536, 128)
    col, row = lane & 127, lane >> 7
    return marks(((col == 0) & (into == 48 + 2 * row)) | ((col == 127) & (into == 49 + 2 * row)))


def tap_table(s, t):
    lane, into = grid(128, 128)
    at = into - OG0
    east, row = at & 1, (at >> 1) + s + 1
    col = jnp.where(east == 1, 128, -1) + t
    near = jnp.where(col == 0, 48 + 2 * row, 49 + 2 * row)
    far = jnp.where(col < 0, 4 * row + col + 2, 4 * row + col - 126)
    given = jnp.where((col == 0) | (col == 127), near, far)
    return marks((at >= 0) & (at < 20) & (lane == given))


def ocean_side_table(east):
    lane, into = grid(128, 128)
    at = lane - OC0
    return marks((at >= 0) & (at < 24) & (into == 4 * (at >> 1) + (at & 1) + 2 * east))


def dot(a, b):
    return jnp.dot(a, b, preferred_element_type=F32)


def dot_last(a, b):
    return lax.dot_general(a, b, (((1,), (1,)), ((), ())), preferred_element_type=F32)


def call(kernel, outs, in_specs, scratch=(), limit=32, cost=1):
    return pl.pallas_call(
        kernel,
        out_shape=[jax.ShapeDtypeStruct(shape, dtype) for shape, dtype in outs],
        in_specs=list(in_specs),
        out_specs=[VMEM] * len(outs),
        scratch_shapes=list(scratch),
        compiler_params=pltpu.CompilerParams(vmem_limit_bytes=limit << 20),
        cost_estimate=pl.CostEstimate(flops=cost * 10**9, bytes_accessed=cost * 3 * 10**6, transcendentals=0),
    )


def parcels_kernel(sends, ocean, *outs):
    tile = lax.axis_index("tile")
    facing = 1 - 2 * (tile & 1)

    def parcel(out, at, shift):
        target = (tile + HALF + shift) & (TILES - 1)
        for slot in range(3):
            block = sends[slot, 0, target]
            start = pl.multiple_of(jnp.maximum(block, 0) * LANES, LANES)
            data = ocean[:, pl.ds(start, LANES)]
            out[at + 32 * slot : at + 32 * slot + 32, :] = jnp.where(block >= 0, data, jnp.zeros_like(data))

    for step, out in zip(CHIP_STEPS, outs):
        parcel(out, 0, 2 * step)
        parcel(out, 96, 2 * step + facing)
    parcel(outs[3], 0, -3 * facing)


def copies_kernel(atm, grad, copies):
    for chan in range(4):
        copies[chan, 0:64] = atm[...]
        copies[chan, 64:128] = grad[...]


def regrid_kernel(sources, blocks, a0, a1, a2, crossed, far, weights, atm, grad, regridded, north, south, sides, held, acc):
    tile = lax.axis_index("tile")
    facing = 1 - 2 * (tile & 1)
    for i, ref in enumerate((a0, a1, a2)):
        held[96 * i : 96 * i + 96, :] = ref[0:96, :]
    held[288:576, :] = crossed[0:288, :]
    held[576:672, :] = far[...]
    acc[...] = jnp.zeros_like(acc)
    for k in range(4):
        shift = ((sources[0, k] - tile - HALF + 3 + 2 * TILES) & (TILES - 1)) - 3
        odd = shift & 1
        even_at = 1 - (shift >> 1)
        odd_at = jnp.where(shift == -3 * facing, 6, 4 + ((facing - shift) >> 1))
        at = jnp.clip(jnp.where(odd == 1, odd_at, even_at), 0, 6)
        for slot in range(3):
            block = blocks[0, 3 * k + slot]

            @pl.when(block >= 0)
            def _():
                rows = pl.ds(pl.multiple_of(at * 96 + 32 * slot, 32), 32)
                into = pl.ds(pl.multiple_of(block * 32, 32), 32)
                acc[into, :] += dot(held[rows, :], weights[3 * k + slot])

    for a in range(8):
        regridded[:, LANES * a : LANES * (a + 1)] = acc[32 * a : 32 * (a + 1), :].astype(BF)
    north[:, 0:256] = atm[:, 0:256]
    north[:, 256:384] = grad[:, 0:128]
    north[0:32, 384:512] = regridded[:, 0:128]
    north[32:64, 384:512] = regridded[:, 128:256]
    south[:, 0:256] = atm[:, 768:1024]
    south[:, 256:384] = grad[:, 896:1024]
    south[0:32, 384:512] = regridded[:, 768:896]
    south[32:64, 384:512] = regridded[:, 896:1024]
    edges = dot(atm[...], edge_table(0)) + dot(grad[...], grad_edge_table())
    sides[0:32, :] = (edges[0:32] + dot(regridded[...], edge_table(64))).astype(BF)
    sides[32:64, :] = edges[32:64].astype(BF)


def select_kernel(own_near, mate_near, gathered, regridded, bias, own, mate):
    core = lax.axis_index("tile") & 1
    for near, out in ((own_near, own), (mate_near, mate)):

        def pick(direction):
            device = near[0, direction]
            here = (device >= 0) & ((device & 1) == core)
            chip = (device & 7) >> 1
            return jnp.where(here, chip, 0), here

        def strip(direction, lanes):
            chip, here = pick(direction)
            data = gathered[chip, :, lanes[0] : lanes[1]]
            return jnp.where(here, data, jnp.zeros_like(data))

        out[:, 0:512] = strip(0, (0, 512))
        out[:, 512:1024] = strip(1, (512, 1024))
        total = jnp.zeros((64, 128), F32)
        halves = [jnp.zeros((32, 128), F32), jnp.zeros((32, 128), F32)]
        for east in (0, 1):
            data = strip(2 + east, (1024, 1152))
            given = 0 if east else 16
            picks = beside_table(given, 8 + 2 * east, 4) + beside_grad_table(32 if east else 40, OG0 + 2 + east)
            total = total + dot(data, picks)
            halves[east] = halves[east] + dot(data[0:32], beside_table(64 + given, OC0 + 4, 2))
            col = 0 if east else 126
            for at_south in (0, 1):
                first, beyond = (10, 9) if at_south else (0, 0)
                data = strip(4 + 2 * at_south + east, (512, 1024) if at_south else (0, 512))
                for q in (0, 1):
                    total = total + dot(data[:, 128 * q : 128 * q + 128], pair_table(col, 4 * (first + q) + 2 * east))
                    halves[east] = halves[east] + dot(data[32 * q : 32 * q + 32, 384:512], pair_table(col, OC0 + 2 * (first + q)))
                total = total + dot(data[:, 256:384], single_table(0 if east else 127, OG0 + 2 * beyond + east))
        out[0:32, 1024:1152] = (total[0:32] + halves[0]).astype(BF)
        out[32:64, 1024:1152] = (total[32:64] + halves[1]).astype(BF)
    side = own[:, 1024:1152].astype(F32)
    row, _ = grid(64, 64)
    _, lane = grid(64, 128)
    rest = jnp.sum(jnp.where(row == lane[:, 0:64], bias[...], 0.0), axis=1, keepdims=True)
    for i in range(3):
        part = rest.astype(BF).astype(F32)
        side = jnp.where(lane == BIAS0 + i, part, side)
        rest = rest - part
    own[:, 1024:1152] = side.astype(BF)
    own[0:32, 1152:1664] = regridded[:, 0:512]
    own[32:64, 1152:1664] = regridded[:, 512:1024]


def forward_kernel(
    inner, outer_held, flipped, output, z_all, mine, theirs, side_atm, taps, side_taps, grads, outs, weights, outer, lifted, sems
):
    chan, core = lax.axis_index("chan"), lax.axis_index("tile") & 1
    fetches = [pltpu.make_async_copy(outer_held, outer, sems.at[0])]
    for c in range(4):
        own = slice(64 * c, 64 * c + 64)
        state = taps.at[pl.ds(384 + 64 * c, 64), pl.ds(256, 1024)]
        fetches.append(pltpu.make_async_copy(inner.at[c, pl.ds(0, 64)], state, sems.at[1 + c]))
        fetches.append(pltpu.make_async_copy(inner.at[c, pl.ds(64, 64)], grads.at[own, pl.ds(128, 1024)], sems.at[5 + c]))
    fetches.append(pltpu.make_async_copy(flipped, weights, sems.at[9]))
    for fetch in fetches:
        fetch.start()
    fetches[0].wait()
    _, lane = grid(64, 128)
    for c in range(4):
        atm = slice(64 * c, 64 * c + 64)
        mid = slice(384 + 64 * c, 448 + 64 * c)
        sea = slice(640 + 32 * c, 672 + 32 * c)
        taps[mid, 0:256] = outer[c, :, 0:256]
        taps[mid, 1280:1536] = outer[c, :, 512:768]
        side_atm[atm, :] = outer[c, :, 1024:1152]
        taps[sea, 0:128] = outer[c, 0:32, 384:512]
        taps[sea, 128:256] = outer[c, 32:64, 384:512]
        taps[sea, 256:768] = outer[c, 0:32, 1152:1664]
        taps[sea, 768:1280] = outer[c, 32:64, 1152:1664]
        taps[sea, 1280:1408] = outer[c, 0:32, 896:1024]
        taps[sea, 1408:1536] = outer[c, 32:64, 896:1024]
        side = dot(outer[c, 0:32, 1024:1152], ocean_side_table(0)) + dot(outer[c, 32:64, 1024:1152], ocean_side_table(1))
        side_atm[256 + 32 * c : 288 + 32 * c, :] = side.astype(BF)
        grads[atm, 0:128] = outer[c, :, 256:384]
        grads[atm, 1152:1280] = outer[c, :, 768:896]
        side = outer[c, :, 1024:1152]
        grads[atm, 1280:1408] = jnp.where((lane >= OG0) & (lane < OC0), side, jnp.zeros_like(side))
    for fetch in fetches[1:9]:
        fetch.wait()
    side = side_atm[...]
    shifts, edges = shift_tables(), edge_rows()
    for r in range(12):
        lanes = slice(128 * r, 128 * r + 128)
        table = jnp.concatenate([shifts, edge_marks(edges, 4 * r + 1)], axis=0)
        moved = dot(jnp.concatenate([taps[384:768, lanes], side], axis=1), table).astype(BF)
        taps[0:384, lanes] = moved[:, 0:128]
        taps[768:1152, lanes] = moved[:, 128:256]
    _, lane = grid(384, 128)
    columns = dot(taps[384:768, :], gather_table()).astype(BF)
    columns = jnp.where(lane < 48, side, columns)
    moved = dot(columns, jnp.concatenate([tap_table(s, t) for s in (-1, 0, 1) for t in (-1, 0, 1)], axis=1)).astype(BF)
    for s in range(3):
        for t in range(3):
            at = 128 * (3 * s + t)
            side_taps[384 * t : 384 * t + 384, 128 * s : 128 * s + 128] = moved[:, at : at + 128]
    bias = jnp.concatenate(
        [jnp.sum(outer[c, :, 1024 + BIAS0 : 1024 + BIAS0 + 3].astype(F32), axis=1, keepdims=True) for c in range(4)], axis=0
    )

    fetches[9].wait()

    def activate(total, lanes):
        pre = total + bias
        gate = 1.0 / (1.0 + jnp.exp(-pre))
        z_all[:, lanes] = (grads[:, lanes].astype(F32) * gate * (1.0 + pre * (1.0 - gate))).astype(BF)
        return pre * gate

    for r in range(0, 10, 2):
        total = jnp.zeros((256, 256), F32)
        for s in range(3):
            total = total + dot(weights[s], taps[:, 128 * (r + s) : 128 * (r + s) + 256])
        silu = activate(total, slice(128 * r, 128 * r + 256))
        for q in (0, 1):
            row = r + q - 1
            if 0 <= row < 8:
                state = taps[384:640, 128 * (row + 2) : 128 * (row + 3)].astype(F32)
                outs[:, 128 * row : 128 * row + 128] = (state + silu[:, 128 * q : 128 * q + 128]).astype(BF)
    total = jnp.zeros((256, 128), F32)
    for s in range(3):
        total = total + dot(weights[s], side_taps[:, 128 * s : 128 * s + 128])
    activate(total, slice(1280, 1408))
    rows = pl.ds(pl.multiple_of(chan * 64, 64), 64)
    output[...] = outs[rows, :]
    own = z_all[rows, 128:1152]
    sums = dot_last(jnp.ones((16, 1024), BF), own)
    for half, first in ((0, mine), (1, theirs)):
        first[54:64] = jnp.zeros((10, 16, 128), first.dtype)
        first[54, :, 0:64] = sums.astype(first.dtype)
    lifted[...] = jnp.zeros_like(lifted)
    for s in range(3):
        lifted[64 * s : 64 * s + 64, 128 * (s + 1) : 128 * (s + 1) + 1024] = own
    found = dot_last(lifted[...], taps[...])
    for s in range(3):
        for t in range(3):
            for a in range(4):
                for l in range(3):
                    piece = found[64 * s + 16 * a : 64 * s + 16 * a + 16, 384 * t + 128 * l : 384 * t + 128 * l + 128]
                    row = 4 * (3 * s + t) + a
                    half, at = row // 18, (row % 18) * 3 + l

                    @pl.when(core == half)
                    def _():
                        mine[at] = piece

                    @pl.when(core != half)
                    def _():
                        theirs[at] = piece.astype(BF)


def backward_kernel(
    sources, blocks, z_all, weights_held, regrid_weights, grad,
    input_grad, r0, r1, r2, far, taps, delta, terms, weights, sem,
):
    fetch = pltpu.make_async_copy(weights_held, weights, sem)
    fetch.start()
    tile, chan = lax.axis_index("tile"), lax.axis_index("chan")
    facing = 1 - 2 * (tile & 1)
    side = z_all[:, 1280:1408]
    shifts, edges = shift_tables(), edge_rows()
    for r in range(10):
        lanes = slice(128 * r, 128 * r + 128)
        table = jnp.concatenate([shifts, edge_marks(edges, OG0 + 2 * r)], axis=0)
        moved = dot(jnp.concatenate([z_all[:, lanes], side], axis=1), table).astype(BF)
        taps[512:768, lanes] = moved[:, 0:128]
        taps[0:256, lanes] = moved[:, 128:256]
    taps[256:512, :] = z_all[:, 0:1280]
    atm_rows = pl.ds(pl.multiple_of(chan * 64, 64), 64)
    sea_rows = pl.ds(pl.multiple_of(256 + chan * 32, 32), 32)
    fetch.wait()
    for q in range(4):
        atm_total = jnp.zeros((64, 256), F32)
        sea_total = jnp.zeros((32, 256), F32)
        for s in range(3):
            first = 128 * (2 * q + 2 - s)
            for t in range(3):
                window = taps[256 * t : 256 * t + 256, first : first + 256]
                atm_total = atm_total + dot(weights[3 * s + t, atm_rows, :], window)
                sea_total = sea_total + dot(weights[3 * s + t, sea_rows, :], window)
        lanes = slice(256 * q, 256 * q + 256)
        input_grad[:, lanes] = (grad[:, lanes].astype(F32) + atm_total).astype(BF)
        delta[:, lanes] = sea_total.astype(BF)
    for e in range(12):
        block = blocks[0, e]
        lanes = pl.ds(pl.multiple_of(jnp.maximum(block, 0) * LANES, LANES), LANES)
        term = dot_last(delta[:, lanes], regrid_weights[e])
        terms[32 * e : 32 * e + 32, :] = jnp.where(block >= 0, term, 0.0).astype(BF)
    terms[384:480, :] = jnp.zeros((96, 128), BF)

    def parcel(out, at, shift):
        target = (tile + HALF + shift) & (TILES - 1)
        found = jnp.int32(4)
        for k in range(4):
            found = jnp.where(sources[0, k] == target, k, found)
        out[at : at + 96, :] = terms[pl.ds(pl.multiple_of(found * 96, 96), 96), :]

    for step, out in zip(CHIP_STEPS, (r0, r1, r2)):
        parcel(out, 0, 2 * step)
        parcel(out, 96, 2 * step + facing)
    parcel(far, 0, -3 * facing)


def return_kernel(sends, a0, a1, a2, crossed, far, ocean_grad, acc):
    tile = lax.axis_index("tile")
    facing = 1 - 2 * (tile & 1)
    acc[...] = jnp.zeros_like(acc)

    def add(ref, first, shift):
        sender = (tile + HALF + shift) & (TILES - 1)
        for slot in range(3):
            block = sends[slot, 0, sender]

            @pl.when(block >= 0)
            def _():
                into = pl.ds(pl.multiple_of(block * 32, 32), 32)
                acc[into, :] += ref[first + 32 * slot : first + 32 * slot + 32, :].astype(F32)

    for i, (step, ref) in enumerate(zip(CHIP_STEPS, (a0, a1, a2))):
        add(ref, 0, -2 * step)
        add(crossed, 96 * i, -2 * step + facing)
    add(far, 0, -3 * facing)
    for b in range(8):
        ocean_grad[:, LANES * b : LANES * (b + 1)] = acc[32 * b : 32 * (b + 1), :]


def add_kernel(mine, crossed, total):
    total[...] = (mine[...] + crossed[...].astype(F32)).astype(BF)


def sum_kernel(scale, arrived, out):
    total = (jnp.sum(arrived[...].astype(F32), axis=0) * scale).astype(BF)
    for i in range(64):
        out[i] = total


def finish_kernel(held, crossed, weight_grad):
    core = lax.axis_index("tile") & 1
    for half in range(2):
        for a in range(18):
            row = 18 * half + a
            k, part = row // 4, row % 4
            for l in range(3):
                at = 3 * a + l
                piece = jnp.where(core == half, held[at].astype(F32), crossed[at].astype(F32))
                weight_grad[k, 16 * part : 16 * part + 16, 128 * l : 128 * l + 128] = piece


def send(array, target):
    return lax.ppermute(array, "tile", [(i, target(i)) for i in range(TILES)])


def chip_send(array, at):
    return send(array, lambda i: (i + HALF + 2 * CHIP_STEPS[at]) % TILES)


def far_send(array):
    return send(array, lambda i: (i + HALF - 3 * (1 - 2 * (i % 2))) % TILES)


def to_mate(array):
    return send(array, lambda i: i ^ 1)


def on_device(
    atm_state,
    ocean_state,
    conv_weight,
    conv_bias,
    regrid_weight,
    out_grad,
    atm_neighbours,
    coupling_sources,
    coupling_blocks,
    coupling_sends,
):
    sends = jnp.transpose(coupling_sends, (2, 0, 1))
    flipped = jnp.swapaxes(conv_weight.reshape(3, 1152, 256), 1, 2)
    b0, b1, b2, far = call(parcels_kernel, [((192, 128), BF)] * 3 + [((96, 128), BF)], [SMEM, VMEM])(sends, ocean_state)
    (copies,) = call(copies_kernel, [((4, 128, 1024), BF)], [VMEM, VMEM])(atm_state, out_grad)
    inner = lax.all_to_all(copies, "chan", 0, 0)
    a0, a1, a2, far = chip_send(b0, 0), chip_send(b1, 1), chip_send(b2, 2), far_send(far)
    far, flipped = lax.optimization_barrier((far, flipped))
    table = jnp.pad(atm_neighbours.astype(BF), ((0, 15), (0, 120)))
    crossed = to_mate(jnp.concatenate([a0[96:], a1[96:], a2[96:], table], axis=0))
    mate_near = crossed[288:289, 0:8].astype(jnp.int32)
    regridded, north, south, sides = call(
        regrid_kernel,
        [((32, 1024), BF), ((64, 512), BF), ((64, 512), BF), ((64, 128), BF)],
        [SMEM] * 2 + [VMEM] * 8,
        [pltpu.VMEM((672, 128), BF), pltpu.VMEM((256, 128), F32)],
    )(coupling_sources, coupling_blocks, a0, a1, a2, crossed, far, regrid_weight, atm_state, out_grad)
    from_north = lax.ppermute(south, "tile", [(i, i + 8) for i in range(TILES - 8)])
    from_south = lax.ppermute(north, "tile", [(i + 8, i) for i in range(TILES - 8)])
    strips = jnp.concatenate([from_north, from_south, sides], axis=1)
    strips, inner = lax.optimization_barrier((strips, inner))
    strips = lax.all_gather(strips, "tile", axis_index_groups=ROW_CHIPS)
    own, mate = call(select_kernel, [((64, 1664), BF), ((64, 1152), BF)], [SMEM] * 2 + [VMEM] * 3)(
        atm_neighbours, mate_near, strips, regridded, conv_bias.reshape(1, 64)
    )
    shard = own + jnp.pad(to_mate(mate), ((0, 0), (0, 512)))
    outer = lax.all_gather(shard, "chan")
    atm_output, z_all, mine, theirs = call(
        forward_kernel,
        [((64, 1024), BF), ((256, 1408), BF), ((64, 16, 128), F32), ((64, 16, 128), BF)],
        [HELD] * 3,
        [
            pltpu.VMEM((384, 128), BF),
            pltpu.VMEM((1152, 1536), BF),
            pltpu.VMEM((1152, 384), BF),
            pltpu.VMEM((256, 1408), BF),
            pltpu.VMEM((256, 1024), BF),
            pltpu.VMEM((3, 256, 1152), BF),
            pltpu.VMEM((4, 64, 1664), BF),
            pltpu.VMEM((192, 1536), BF),
            pltpu.SemaphoreType.DMA((10,)),
        ],
        limit=56,
        cost=10,
    )(inner, outer, flipped)
    (total,) = call(add_kernel, [((64, 16, 128), BF)], [VMEM, VMEM])(mine, to_mate(theirs))
    total, z_all = lax.optimization_barrier((total, z_all))
    shares = lax.all_to_all(total, "tile", 0, 0, axis_index_groups=SAME_CORE)
    input_grad, b0, b1, b2, far = call(
        backward_kernel,
        [((64, 1024), BF)] + [((192, 128), BF)] * 3 + [((96, 128), BF)],
        [SMEM] * 2 + [VMEM, HELD, VMEM, VMEM],
        [
            pltpu.VMEM((768, 1280), BF),
            pltpu.VMEM((32, 1024), BF),
            pltpu.VMEM((480, 128), BF),
            pltpu.VMEM((9, 384, 256), BF),
            pltpu.SemaphoreType.DMA,
        ],
        limit=48,
        cost=4,
    )(coupling_sources, coupling_blocks, z_all, conv_weight, regrid_weight, out_grad)
    a0, a1, a2 = chip_send(b0, 0), chip_send(b1, 1), chip_send(b2, 2)
    shares, a0, a1, far = lax.optimization_barrier((shares, a0, a1, far))
    scale = 1.0 / math.sqrt(atm_state.shape[1] * TILES)
    (summed,) = call(functools.partial(sum_kernel, scale), [((64, 16, 128), BF)], [VMEM])(shares)
    summed, far = lax.optimization_barrier((summed, far))
    held = lax.all_to_all(summed, "tile", 0, 0, axis_index_groups=SAME_CORE)
    far = far_send(far)
    a2, far = lax.optimization_barrier((a2, far))
    crossed = to_mate(jnp.concatenate([a0[96:], a1[96:], a2[96:]], axis=0))
    (ocean_grad,) = call(return_kernel, [((32, 1024), F32)], [SMEM] + [VMEM] * 5, [pltpu.VMEM((256, 128), F32)])(
        sends, a0, a1, a2, crossed, far
    )
    held, ocean_grad = lax.optimization_barrier((held, ocean_grad))
    crossed = to_mate(held)
    bias_grad = held[54, 0, 0:64].astype(F32)
    (weight_grad,) = call(finish_kernel, [((9, 64, 384), F32)], [VMEM, VMEM])(held, crossed)
    return atm_output, input_grad, ocean_grad, jnp.swapaxes(weight_grad, 1, 2), bias_grad


def solution(mesh):
    placed = (
        P("chan", "tile"),
        P("chan", "tile"),
        P(),
        P("chan"),
        P("tile", None, None),
        P("chan", "tile"),
        P("tile", None),
        P("tile", None),
        P("tile", None),
        P("tile", None, None),
    )
    return jax.shard_map(
        on_device,
        mesh=mesh,
        in_specs=placed,
        out_specs=(
            P("chan", "tile"),
            P("chan", "tile"),
            P("chan", "tile"),
            P(None, None, "chan"),
            P("chan"),
        ),
        check_vma=False,
    )
```

```python
import functools
import math

import jax
import jax.numpy as jnp
from jax import lax
from jax.experimental import pallas as pl
from jax.experimental.pallas import tpu as pltpu
from jax.sharding import PartitionSpec as P

BF, F32 = jnp.bfloat16, jnp.float32
TILES = 128
HALF = TILES // 2
LANES = 128
OG0, OC0, BIAS0 = 48, 68, 92
VMEM = pl.BlockSpec(memory_space=pltpu.VMEM)
SMEM = pl.BlockSpec(memory_space=pltpu.SMEM)
HELD = pl.BlockSpec(memory_space=pl.ANY)

CHIP_STEPS = (-1, 0, 1)
ROW_CHIPS = [[8 * r + 2 * i + c for i in range(4)] for r in range(16) for c in range(2)]
SAME_CORE = [[2 * i + c for i in range(64)] for c in range(2)]


def grid(rows, columns):
    shape = (rows, columns)
    return lax.broadcasted_iota(jnp.int32, shape, 0), lax.broadcasted_iota(jnp.int32, shape, 1)


def marks(where):
    return jnp.where(where, 1.0, 0.0).astype(BF)


def edge_table(first):
    cell, lane = grid(1024, 128)
    col, at = cell & 127, first + 2 * (cell >> 7)
    return marks(((col < 2) & (lane == at + col)) | ((col >= 126) & (lane == at + col - 110)))


def grad_edge_table():
    cell, lane = grid(1024, 128)
    col, row = cell & 127, cell >> 7
    return marks(((col == 0) & (lane == 32 + row)) | ((col == 127) & (lane == 40 + row)))


def pair_table(given, to):
    lane, into = grid(128, 128)
    return marks((lane >= given) & (lane < given + 2) & (into - to == lane - given))


def single_table(given, to):
    lane, into = grid(128, 128)
    return marks((lane == given) & (into == to))


def beside_table(given, to, step):
    lane, into = grid(128, 128)
    at = lane - given
    return marks((at >= 0) & (at < 16) & (into == to + step * (at >> 1) + (at & 1)))


def beside_grad_table(given, to):
    lane, into = grid(128, 128)
    at = lane - given
    return marks((at >= 0) & (at < 8) & (into == to + 2 * at))


def shift_table(step):
    lane, into = grid(128, 128)
    return marks(lane == into + step)


def shift_tables():
    return jnp.concatenate([shift_table(-1), shift_table(1)], axis=1)


def edge_rows():
    lane, into = grid(128, 256)
    return jnp.where(into == 0, lane, jnp.where(into == 255, lane - 1, -8))


def edge_marks(rows, first):
    return marks(rows == first)


def gather_table():
    lane, into = grid(1536, 128)
    col, row = lane & 127, lane >> 7
    return marks(((col == 0) & (into == 48 + 2 * row)) | ((col == 127) & (into == 49 + 2 * row)))


def tap_table(s, t):
    lane, into = grid(128, 128)
    at = into - OG0
    east, row = at & 1, (at >> 1) + s + 1
    col = jnp.where(east == 1, 128, -1) + t
    near = jnp.where(col == 0, 48 + 2 * row, 49 + 2 * row)
    far = jnp.where(col < 0, 4 * row + col + 2, 4 * row + col - 126)
    given = jnp.where((col == 0) | (col == 127), near, far)
    return marks((at >= 0) & (at < 20) & (lane == given))


def ocean_side_table(east):
    lane, into = grid(128, 128)
    at = lane - OC0
    return marks((at >= 0) & (at < 24) & (into == 4 * (at >> 1) + (at & 1) + 2 * east))


def dot(a, b):
    return jnp.dot(a, b, preferred_element_type=F32)


def dot_last(a, b):
    return lax.dot_general(a, b, (((1,), (1,)), ((), ())), preferred_element_type=F32)


def call(kernel, outs, in_specs, scratch=(), limit=32, cost=1):
    return pl.pallas_call(
        kernel,
        out_shape=[jax.ShapeDtypeStruct(shape, dtype) for shape, dtype in outs],
        in_specs=list(in_specs),
        out_specs=[VMEM] * len(outs),
        scratch_shapes=list(scratch),
        compiler_params=pltpu.CompilerParams(vmem_limit_bytes=limit << 20),
        cost_estimate=pl.CostEstimate(flops=cost * 10**9, bytes_accessed=cost * 3 * 10**6, transcendentals=0),
    )


def parcels_kernel(sends, ocean, *outs):
    tile = lax.axis_index("tile")
    facing = 1 - 2 * (tile & 1)

    def parcel(out, at, shift):
        target = (tile + HALF + shift) & (TILES - 1)
        for slot in range(3):
            block = sends[slot, 0, target]
            start = pl.multiple_of(jnp.maximum(block, 0) * LANES, LANES)
            data = ocean[:, pl.ds(start, LANES)]
            out[at + 32 * slot : at + 32 * slot + 32, :] = jnp.where(block >= 0, data, jnp.zeros_like(data))

    for step, out in zip(CHIP_STEPS, outs):
        parcel(out, 0, 2 * step)
        parcel(out, 96, 2 * step + facing)
    parcel(outs[3], 0, -3 * facing)


def copies_kernel(atm, grad, copies):
    for chan in range(4):
        copies[chan, 0:64] = atm[...]
        copies[chan, 64:128] = grad[...]


def regrid_kernel(sources, blocks, a0, a1, a2, crossed, far, weights, atm, grad, regridded, keep, give, sides, held, acc):
    tile = lax.axis_index("tile")
    facing = 1 - 2 * (tile & 1)
    for i, ref in enumerate((a0, a1, a2)):
        held[96 * i : 96 * i + 96, :] = ref[0:96, :]
    held[288:576, :] = crossed[0:288, :]
    held[576:672, :] = far[...]
    acc[...] = jnp.zeros_like(acc)
    for k in range(4):
        shift = ((sources[0, k] - tile - HALF + 3 + 2 * TILES) & (TILES - 1)) - 3
        odd = shift & 1
        even_at = 1 - (shift >> 1)
        odd_at = jnp.where(shift == -3 * facing, 6, 4 + ((facing - shift) >> 1))
        at = jnp.clip(jnp.where(odd == 1, odd_at, even_at), 0, 6)
        for slot in range(3):
            block = blocks[0, 3 * k + slot]

            @pl.when(block >= 0)
            def _():
                rows = pl.ds(pl.multiple_of(at * 96 + 32 * slot, 32), 32)
                into = pl.ds(pl.multiple_of(block * 32, 32), 32)
                acc[into, :] += dot(held[rows, :], weights[3 * k + slot])

    for a in range(8):
        regridded[:, LANES * a : LANES * (a + 1)] = acc[32 * a : 32 * (a + 1), :].astype(BF)

    def north(out):
        out[:, 0:256] = atm[:, 0:256]
        out[:, 256:384] = grad[:, 0:128]
        out[0:32, 384:512] = regridded[:, 0:128]
        out[32:64, 384:512] = regridded[:, 128:256]

    def south(out):
        out[:, 0:256] = atm[:, 768:1024]
        out[:, 256:384] = grad[:, 896:1024]
        out[0:32, 384:512] = regridded[:, 768:896]
        out[32:64, 384:512] = regridded[:, 896:1024]

    @pl.when(facing == 1)
    def _():
        south(keep)
        north(give)

    @pl.when(facing != 1)
    def _():
        north(keep)
        south(give)

    edges = dot(atm[...], edge_table(0)) + dot(grad[...], grad_edge_table())
    sides[0:32, :] = (edges[0:32] + dot(regridded[...], edge_table(64))).astype(BF)
    sides[32:64, :] = edges[32:64].astype(BF)


def select_kernel(own_near, mate_near, gathered, regridded, bias, own, mate):
    core = lax.axis_index("tile") & 1
    for near, out in ((own_near, own), (mate_near, mate)):

        def strip(direction):
            device = near[0, direction]
            side = 1 if direction in (1, 6, 7) else 0
            here = (device >= 0) & (core == side)
            first = pl.multiple_of(jnp.where(here, (device & 1) ^ side, 0) * 512, 512)
            data = gathered[jnp.where(here, (device & 7) >> 1, 0), :, pl.ds(first, 512)]
            return jnp.where(here, data, jnp.zeros_like(data))

        def beside(direction):
            device = near[0, direction]
            here = (device >= 0) & ((device & 1) == core)
            data = gathered[jnp.where(here, (device & 7) >> 1, 0), :, 1024:1152]
            return jnp.where(here, data, jnp.zeros_like(data))

        out[:, 0:512] = strip(0)
        out[:, 512:1024] = strip(1)
        total = jnp.zeros((64, 128), F32)
        halves = [jnp.zeros((32, 128), F32), jnp.zeros((32, 128), F32)]
        for east in (0, 1):
            data = beside(2 + east)
            given = 0 if east else 16
            picks = beside_table(given, 8 + 2 * east, 4) + beside_grad_table(32 if east else 40, OG0 + 2 + east)
            total = total + dot(data, picks)
            halves[east] = halves[east] + dot(data[0:32], beside_table(64 + given, OC0 + 4, 2))
            col = 0 if east else 126
            for at_south in (0, 1):
                first, beyond = (10, 9) if at_south else (0, 0)
                data = strip(4 + 2 * at_south + east)
                for q in (0, 1):
                    total = total + dot(data[:, 128 * q : 128 * q + 128], pair_table(col, 4 * (first + q) + 2 * east))
                    halves[east] = halves[east] + dot(data[32 * q : 32 * q + 32, 384:512], pair_table(col, OC0 + 2 * (first + q)))
                total = total + dot(data[:, 256:384], single_table(0 if east else 127, OG0 + 2 * beyond + east))
        out[0:32, 1024:1152] = (total[0:32] + halves[0]).astype(BF)
        out[32:64, 1024:1152] = (total[32:64] + halves[1]).astype(BF)
    side = own[:, 1024:1152].astype(F32)
    row, _ = grid(64, 64)
    _, lane = grid(64, 128)
    rest = jnp.sum(jnp.where(row == lane[:, 0:64], bias[...], 0.0), axis=1, keepdims=True)
    for i in range(3):
        part = rest.astype(BF).astype(F32)
        side = jnp.where(lane == BIAS0 + i, part, side)
        rest = rest - part
    own[:, 1024:1152] = side.astype(BF)
    own[0:32, 1152:1664] = regridded[:, 0:512]
    own[32:64, 1152:1664] = regridded[:, 512:1024]


def forward_kernel(
    inner, outer_held, flipped, output, z_all, mine, theirs, side_atm, taps, side_taps, grads, outs, weights, outer, lifted, sems
):
    chan, core = lax.axis_index("chan"), lax.axis_index("tile") & 1
    fetches = [pltpu.make_async_copy(outer_held, outer, sems.at[0])]
    for c in range(4):
        own = slice(64 * c, 64 * c + 64)
        state = taps.at[pl.ds(384 + 64 * c, 64), pl.ds(256, 1024)]
        fetches.append(pltpu.make_async_copy(inner.at[c, pl.ds(0, 64)], state, sems.at[1 + c]))
        fetches.append(pltpu.make_async_copy(inner.at[c, pl.ds(64, 64)], grads.at[own, pl.ds(128, 1024)], sems.at[5 + c]))
    fetches.append(pltpu.make_async_copy(flipped, weights, sems.at[9]))
    for fetch in fetches:
        fetch.start()
    fetches[0].wait()
    _, lane = grid(64, 128)
    for c in range(4):
        atm = slice(64 * c, 64 * c + 64)
        mid = slice(384 + 64 * c, 448 + 64 * c)
        sea = slice(640 + 32 * c, 672 + 32 * c)
        taps[mid, 0:256] = outer[c, :, 0:256]
        taps[mid, 1280:1536] = outer[c, :, 512:768]
        side_atm[atm, :] = outer[c, :, 1024:1152]
        taps[sea, 0:128] = outer[c, 0:32, 384:512]
        taps[sea, 128:256] = outer[c, 32:64, 384:512]
        taps[sea, 256:768] = outer[c, 0:32, 1152:1664]
        taps[sea, 768:1280] = outer[c, 32:64, 1152:1664]
        taps[sea, 1280:1408] = outer[c, 0:32, 896:1024]
        taps[sea, 1408:1536] = outer[c, 32:64, 896:1024]
        side = dot(outer[c, 0:32, 1024:1152], ocean_side_table(0)) + dot(outer[c, 32:64, 1024:1152], ocean_side_table(1))
        side_atm[256 + 32 * c : 288 + 32 * c, :] = side.astype(BF)
        grads[atm, 0:128] = outer[c, :, 256:384]
        grads[atm, 1152:1280] = outer[c, :, 768:896]
        side = outer[c, :, 1024:1152]
        grads[atm, 1280:1408] = jnp.where((lane >= OG0) & (lane < OC0), side, jnp.zeros_like(side))
    for fetch in fetches[1:9]:
        fetch.wait()
    side = side_atm[...]
    shifts, edges = shift_tables(), edge_rows()
    for r in range(12):
        lanes = slice(128 * r, 128 * r + 128)
        table = jnp.concatenate([shifts, edge_marks(edges, 4 * r + 1)], axis=0)
        moved = dot(jnp.concatenate([taps[384:768, lanes], side], axis=1), table).astype(BF)
        taps[0:384, lanes] = moved[:, 0:128]
        taps[768:1152, lanes] = moved[:, 128:256]
    _, lane = grid(384, 128)
    columns = dot(taps[384:768, :], gather_table()).astype(BF)
    columns = jnp.where(lane < 48, side, columns)
    moved = dot(columns, jnp.concatenate([tap_table(s, t) for s in (-1, 0, 1) for t in (-1, 0, 1)], axis=1)).astype(BF)
    for s in range(3):
        for t in range(3):
            at = 128 * (3 * s + t)
            side_taps[384 * t : 384 * t + 384, 128 * s : 128 * s + 128] = moved[:, at : at + 128]
    bias = jnp.concatenate(
        [jnp.sum(outer[c, :, 1024 + BIAS0 : 1024 + BIAS0 + 3].astype(F32), axis=1, keepdims=True) for c in range(4)], axis=0
    )

    fetches[9].wait()

    def activate(total, lanes):
        pre = total + bias
        gate = 1.0 / (1.0 + jnp.exp(-pre))
        z_all[:, lanes] = (grads[:, lanes].astype(F32) * gate * (1.0 + pre * (1.0 - gate))).astype(BF)
        return pre * gate

    for r in range(0, 10, 2):
        total = jnp.zeros((256, 256), F32)
        for s in range(3):
            total = total + dot(weights[s], taps[:, 128 * (r + s) : 128 * (r + s) + 256])
        silu = activate(total, slice(128 * r, 128 * r + 256))
        for q in (0, 1):
            row = r + q - 1
            if 0 <= row < 8:
                state = taps[384:640, 128 * (row + 2) : 128 * (row + 3)].astype(F32)
                outs[:, 128 * row : 128 * row + 128] = (state + silu[:, 128 * q : 128 * q + 128]).astype(BF)
    total = jnp.zeros((256, 128), F32)
    for s in range(3):
        total = total + dot(weights[s], side_taps[:, 128 * s : 128 * s + 128])
    activate(total, slice(1280, 1408))
    rows = pl.ds(pl.multiple_of(chan * 64, 64), 64)
    output[...] = outs[rows, :]
    own = z_all[rows, 128:1152]
    sums = dot_last(jnp.ones((16, 1024), BF), own)
    for half, first in ((0, mine), (1, theirs)):
        first[54:64] = jnp.zeros((10, 16, 128), first.dtype)
        first[54, :, 0:64] = sums.astype(first.dtype)
    lifted[...] = jnp.zeros_like(lifted)
    for s in range(3):
        lifted[64 * s : 64 * s + 64, 128 * (s + 1) : 128 * (s + 1) + 1024] = own
    found = dot_last(lifted[...], taps[...])
    for s in range(3):
        for t in range(3):
            for a in range(4):
                for l in range(3):
                    piece = found[64 * s + 16 * a : 64 * s + 16 * a + 16, 384 * t + 128 * l : 384 * t + 128 * l + 128]
                    row = 4 * (3 * s + t) + a
                    half, at = row // 18, (row % 18) * 3 + l

                    @pl.when(core == half)
                    def _():
                        mine[at] = piece

                    @pl.when(core != half)
                    def _():
                        theirs[at] = piece.astype(BF)


def backward_kernel(
    sources, blocks, z_all, weights_held, regrid_held, grad_held,
    input_grad, r0, r1, r2, far, taps, delta, terms, weights, regrid_weights, grad, sems,
):
    pairs = ((weights_held, weights), (grad_held, grad), (regrid_held, regrid_weights))
    fetches = [pltpu.make_async_copy(held, ref, sems.at[i]) for i, (held, ref) in enumerate(pairs)]
    for fetch in fetches:
        fetch.start()
    tile, chan = lax.axis_index("tile"), lax.axis_index("chan")
    facing = 1 - 2 * (tile & 1)
    side = z_all[:, 1280:1408]
    shifts, edges = shift_tables(), edge_rows()
    for r in range(10):
        lanes = slice(128 * r, 128 * r + 128)
        table = jnp.concatenate([shifts, edge_marks(edges, OG0 + 2 * r)], axis=0)
        moved = dot(jnp.concatenate([z_all[:, lanes], side], axis=1), table).astype(BF)
        taps[512:768, lanes] = moved[:, 0:128]
        taps[0:256, lanes] = moved[:, 128:256]
    taps[256:512, :] = z_all[:, 0:1280]
    atm_rows = pl.ds(pl.multiple_of(chan * 64, 64), 64)
    sea_rows = pl.ds(pl.multiple_of(256 + chan * 32, 32), 32)
    for fetch in fetches:
        fetch.wait()
    for q in range(4):
        atm_total = jnp.zeros((64, 256), F32)
        sea_total = jnp.zeros((32, 256), F32)
        for s in range(3):
            first = 128 * (2 * q + 2 - s)
            for t in range(3):
                window = taps[256 * t : 256 * t + 256, first : first + 256]
                atm_total = atm_total + dot(weights[3 * s + t, atm_rows, :], window)
                sea_total = sea_total + dot(weights[3 * s + t, sea_rows, :], window)
        lanes = slice(256 * q, 256 * q + 256)
        input_grad[:, lanes] = (grad[:, lanes].astype(F32) + atm_total).astype(BF)
        delta[:, lanes] = sea_total.astype(BF)
    for e in range(12):
        block = blocks[0, e]
        lanes = pl.ds(pl.multiple_of(jnp.maximum(block, 0) * LANES, LANES), LANES)
        term = dot_last(delta[:, lanes], regrid_weights[e])
        terms[32 * e : 32 * e + 32, :] = jnp.where(block >= 0, term, 0.0).astype(BF)
    terms[384:480, :] = jnp.zeros((96, 128), BF)

    def parcel(out, at, shift):
        target = (tile + HALF + shift) & (TILES - 1)
        found = jnp.int32(4)
        for k in range(4):
            found = jnp.where(sources[0, k] == target, k, found)
        out[at : at + 96, :] = terms[pl.ds(pl.multiple_of(found * 96, 96), 96), :]

    for step, out in zip(CHIP_STEPS, (r0, r1, r2)):
        parcel(out, 0, 2 * step)
        parcel(out, 96, 2 * step + facing)
    parcel(far, 0, -3 * facing)


def return_kernel(sends, a0, a1, a2, crossed, far, ocean_grad, acc):
    tile = lax.axis_index("tile")
    facing = 1 - 2 * (tile & 1)
    acc[...] = jnp.zeros_like(acc)

    def add(ref, first, shift):
        sender = (tile + HALF + shift) & (TILES - 1)
        for slot in range(3):
            block = sends[slot, 0, sender]

            @pl.when(block >= 0)
            def _():
                into = pl.ds(pl.multiple_of(block * 32, 32), 32)
                acc[into, :] += ref[first + 32 * slot : first + 32 * slot + 32, :].astype(F32)

    for i, (step, ref) in enumerate(zip(CHIP_STEPS, (a0, a1, a2))):
        add(ref, 0, -2 * step)
        add(crossed, 96 * i, -2 * step + facing)
    add(far, 0, -3 * facing)
    for b in range(8):
        ocean_grad[:, LANES * b : LANES * (b + 1)] = acc[32 * b : 32 * (b + 1), :]


def add_kernel(mine, crossed, total):
    total[...] = (mine[...] + crossed[...].astype(F32)).astype(BF)


def sum_kernel(scale, arrived, out):
    total = (jnp.sum(arrived[...].astype(F32), axis=0) * scale).astype(BF)
    for i in range(64):
        out[i] = total


def finish_kernel(held, crossed, weight_grad):
    core = lax.axis_index("tile") & 1
    for half in range(2):
        for a in range(18):
            row = 18 * half + a
            k, part = row // 4, row % 4
            for l in range(3):
                at = 3 * a + l
                piece = jnp.where(core == half, held[at].astype(F32), crossed[at].astype(F32))
                weight_grad[k, 16 * part : 16 * part + 16, 128 * l : 128 * l + 128] = piece


def send(array, target):
    return lax.ppermute(array, "tile", [(i, target(i)) for i in range(TILES)])


def chip_send(array, at):
    return send(array, lambda i: (i + HALF + 2 * CHIP_STEPS[at]) % TILES)


def far_send(array):
    return send(array, lambda i: (i + HALF - 3 * (1 - 2 * (i % 2))) % TILES)


def to_mate(array):
    return send(array, lambda i: i ^ 1)


def on_device(
    atm_state,
    ocean_state,
    conv_weight,
    conv_bias,
    regrid_weight,
    out_grad,
    atm_neighbours,
    coupling_sources,
    coupling_blocks,
    coupling_sends,
):
    sends = jnp.transpose(coupling_sends, (2, 0, 1))
    b0, b1, b2, far = call(parcels_kernel, [((192, 128), BF)] * 3 + [((96, 128), BF)], [SMEM, VMEM])(sends, ocean_state)
    a0, a1, a2, far = chip_send(b0, 0), chip_send(b1, 1), chip_send(b2, 2), far_send(far)
    a0, a1, a2, far = lax.optimization_barrier((a0, a1, a2, far))
    table = jnp.pad(atm_neighbours.astype(BF), ((0, 15), (0, 120)))
    crossed = to_mate(jnp.concatenate([a0[96:], a1[96:], a2[96:], table], axis=0))
    mate_near = crossed[288:289, 0:8].astype(jnp.int32)
    regridded, keep, give, sides = call(
        regrid_kernel,
        [((32, 1024), BF), ((64, 512), BF), ((64, 512), BF), ((64, 128), BF)],
        [SMEM] * 2 + [VMEM] * 8,
        [pltpu.VMEM((672, 128), BF), pltpu.VMEM((256, 128), F32)],
    )(coupling_sources, coupling_blocks, a0, a1, a2, crossed, far, regrid_weight, atm_state, out_grad)
    got, weights_now, atm_now, grad_now = lax.optimization_barrier((to_mate(give), conv_weight, atm_state, out_grad))
    (copies,) = call(copies_kernel, [((4, 128, 1024), BF)], [VMEM, VMEM])(atm_now, grad_now)
    inner = lax.all_to_all(copies, "chan", 0, 0)
    flipped = jnp.swapaxes(weights_now.reshape(3, 1152, 256), 1, 2)
    pair = jnp.concatenate([keep, got], axis=1)
    pairs = [(i, i + 8 - 16 * (i % 2)) for i in range(TILES)]
    arrived = lax.ppermute(pair, "tile", [(i, j) for i, j in pairs if 0 <= j < TILES])
    strips = jnp.concatenate([arrived, sides], axis=1)
    strips, flipped = lax.optimization_barrier((strips, flipped))
    strips = lax.all_gather(strips, "tile", axis_index_groups=ROW_CHIPS)
    own, mate = call(select_kernel, [((64, 1664), BF), ((64, 1152), BF)], [SMEM] * 2 + [VMEM] * 3)(
        atm_neighbours, mate_near, strips, regridded, conv_bias.reshape(1, 64)
    )
    shard = own + jnp.pad(to_mate(mate), ((0, 0), (0, 512)))
    shard, inner = lax.optimization_barrier((shard, inner))
    outer = lax.all_gather(shard, "chan")
    atm_output, z_all, mine, theirs = call(
        forward_kernel,
        [((64, 1024), BF), ((256, 1408), BF), ((64, 16, 128), F32), ((64, 16, 128), BF)],
        [HELD] * 3,
        [
            pltpu.VMEM((384, 128), BF),
            pltpu.VMEM((1152, 1536), BF),
            pltpu.VMEM((1152, 384), BF),
            pltpu.VMEM((256, 1408), BF),
            pltpu.VMEM((256, 1024), BF),
            pltpu.VMEM((3, 256, 1152), BF),
            pltpu.VMEM((4, 64, 1664), BF),
            pltpu.VMEM((192, 1536), BF),
            pltpu.SemaphoreType.DMA((10,)),
        ],
        limit=56,
        cost=10,
    )(inner, outer, flipped)
    (total,) = call(add_kernel, [((64, 16, 128), BF)], [VMEM, VMEM])(mine, to_mate(theirs))
    total, z_all = lax.optimization_barrier((total, z_all))
    shares = lax.all_to_all(total, "tile", 0, 0, axis_index_groups=SAME_CORE)
    input_grad, b0, b1, b2, far = call(
        backward_kernel,
        [((64, 1024), BF)] + [((192, 128), BF)] * 3 + [((96, 128), BF)],
        [SMEM] * 2 + [VMEM] + [HELD] * 3,
        [
            pltpu.VMEM((768, 1280), BF),
            pltpu.VMEM((32, 1024), BF),
            pltpu.VMEM((480, 128), BF),
            pltpu.VMEM((9, 384, 256), BF),
            pltpu.VMEM((12, 128, 128), BF),
            pltpu.VMEM((64, 1024), BF),
            pltpu.SemaphoreType.DMA((3,)),
        ],
        limit=48,
        cost=4,
    )(coupling_sources, coupling_blocks, z_all, conv_weight, regrid_weight, out_grad)
    a0, a1, a2 = chip_send(b0, 0), chip_send(b1, 1), chip_send(b2, 2)
    shares, a0, a1, far = lax.optimization_barrier((shares, a0, a1, far))
    scale = 1.0 / math.sqrt(atm_state.shape[1] * TILES)
    (summed,) = call(functools.partial(sum_kernel, scale), [((64, 16, 128), BF)], [VMEM])(shares)
    summed, far = lax.optimization_barrier((summed, far))
    held = lax.all_to_all(summed, "tile", 0, 0, axis_index_groups=SAME_CORE)
    far = far_send(far)
    a2, far = lax.optimization_barrier((a2, far))
    crossed = to_mate(jnp.concatenate([a0[96:], a1[96:], a2[96:]], axis=0))
    (ocean_grad,) = call(return_kernel, [((32, 1024), F32)], [SMEM] + [VMEM] * 5, [pltpu.VMEM((256, 128), F32)])(
        sends, a0, a1, a2, crossed, far
    )
    held, ocean_grad = lax.optimization_barrier((held, ocean_grad))
    crossed = to_mate(held)
    bias_grad = held[54, 0, 0:64].astype(F32)
    (weight_grad,) = call(finish_kernel, [((9, 64, 384), F32)], [VMEM, VMEM])(held, crossed)
    return atm_output, input_grad, ocean_grad, jnp.swapaxes(weight_grad, 1, 2), bias_grad


def solution(mesh):
    placed = (
        P("chan", "tile"),
        P("chan", "tile"),
        P(),
        P("chan"),
        P("tile", None, None),
        P("chan", "tile"),
        P("tile", None),
        P("tile", None),
        P("tile", None),
        P("tile", None, None),
    )
    return jax.shard_map(
        on_device,
        mesh=mesh,
        in_specs=placed,
        out_specs=(
            P("chan", "tile"),
            P("chan", "tile"),
            P("chan", "tile"),
            P(None, None, "chan"),
            P("chan"),
        ),
        check_vma=False,
    )
```

```python
import functools
import math

import jax
import jax.numpy as jnp
from jax import lax
from jax.experimental import pallas as pl
from jax.experimental.pallas import tpu as pltpu
from jax.sharding import PartitionSpec as P

BF, F32 = jnp.bfloat16, jnp.float32
TILES = 128
HALF = TILES // 2
LANES = 128
OG0, OC0, BIAS0 = 48, 68, 92
VMEM = pl.BlockSpec(memory_space=pltpu.VMEM)
SMEM = pl.BlockSpec(memory_space=pltpu.SMEM)
HELD = pl.BlockSpec(memory_space=pl.ANY)

CHIP_STEPS = (-1, 0, 1)
ROW_CHIPS = [[8 * r + 2 * i + c for i in range(4)] for r in range(16) for c in range(2)]
SAME_CORE = [[2 * i + c for i in range(64)] for c in range(2)]


def grid(rows, columns):
    shape = (rows, columns)
    return lax.broadcasted_iota(jnp.int32, shape, 0), lax.broadcasted_iota(jnp.int32, shape, 1)


def marks(where):
    return jnp.where(where, 1.0, 0.0).astype(BF)


def edge_table(first):
    cell, lane = grid(1024, 128)
    col, at = cell & 127, first + 2 * (cell >> 7)
    return marks(((col < 2) & (lane == at + col)) | ((col >= 126) & (lane == at + col - 110)))


def grad_edge_table():
    cell, lane = grid(1024, 128)
    col, row = cell & 127, cell >> 7
    return marks(((col == 0) & (lane == 32 + row)) | ((col == 127) & (lane == 40 + row)))


def pair_table(given, to):
    lane, into = grid(128, 128)
    return marks((lane >= given) & (lane < given + 2) & (into - to == lane - given))


def single_table(given, to):
    lane, into = grid(128, 128)
    return marks((lane == given) & (into == to))


def beside_table(given, to, step):
    lane, into = grid(128, 128)
    at = lane - given
    return marks((at >= 0) & (at < 16) & (into == to + step * (at >> 1) + (at & 1)))


def beside_grad_table(given, to):
    lane, into = grid(128, 128)
    at = lane - given
    return marks((at >= 0) & (at < 8) & (into == to + 2 * at))


def shift_table(step):
    lane, into = grid(128, 128)
    return marks(lane == into + step)


def shift_tables():
    return jnp.concatenate([shift_table(-1), shift_table(1)], axis=1)


def edge_rows():
    lane, into = grid(128, 256)
    return jnp.where(into == 0, lane, jnp.where(into == 255, lane - 1, -8))


def edge_marks(rows, first):
    return marks(rows == first)


def gather_table():
    lane, into = grid(1536, 128)
    col, row = lane & 127, lane >> 7
    return marks(((col == 0) & (into == 48 + 2 * row)) | ((col == 127) & (into == 49 + 2 * row)))


def tap_table(s, t):
    lane, into = grid(128, 128)
    at = into - OG0
    east, row = at & 1, (at >> 1) + s + 1
    col = jnp.where(east == 1, 128, -1) + t
    near = jnp.where(col == 0, 48 + 2 * row, 49 + 2 * row)
    far = jnp.where(col < 0, 4 * row + col + 2, 4 * row + col - 126)
    given = jnp.where((col == 0) | (col == 127), near, far)
    return marks((at >= 0) & (at < 20) & (lane == given))


def ocean_side_table(east):
    lane, into = grid(128, 128)
    at = lane - OC0
    return marks((at >= 0) & (at < 24) & (into == 4 * (at >> 1) + (at & 1) + 2 * east))


def dot(a, b):
    return jnp.dot(a, b, preferred_element_type=F32)


def dot_last(a, b):
    return lax.dot_general(a, b, (((1,), (1,)), ((), ())), preferred_element_type=F32)


def call(kernel, outs, in_specs, scratch=(), limit=32, cost=1):
    return pl.pallas_call(
        kernel,
        out_shape=[jax.ShapeDtypeStruct(shape, dtype) for shape, dtype in outs],
        in_specs=list(in_specs),
        out_specs=[VMEM] * len(outs),
        scratch_shapes=list(scratch),
        compiler_params=pltpu.CompilerParams(vmem_limit_bytes=limit << 20),
        cost_estimate=pl.CostEstimate(flops=cost * 10**9, bytes_accessed=cost * 3 * 10**6, transcendentals=0),
    )


def parcels_kernel(sends, ocean, *outs):
    tile = lax.axis_index("tile")
    facing = 1 - 2 * (tile & 1)

    def parcel(out, at, shift):
        target = (tile + HALF + shift) & (TILES - 1)
        for slot in range(3):
            block = sends[slot, 0, target]
            start = pl.multiple_of(jnp.maximum(block, 0) * LANES, LANES)
            data = ocean[:, pl.ds(start, LANES)]
            out[at + 32 * slot : at + 32 * slot + 32, :] = jnp.where(block >= 0, data, jnp.zeros_like(data))

    for step, out in zip(CHIP_STEPS, outs):
        parcel(out, 0, 2 * step)
        parcel(out, 96, 2 * step + facing)
    parcel(outs[3], 0, -3 * facing)


def copies_kernel(atm, grad, regridded, copies):
    for chan in range(4):
        copies[chan, 0:64] = atm[...]
        copies[chan, 64:128] = grad[...]
        copies[chan, 128:160] = regridded[...]


def edges_kernel(atm, grad, edges):
    edges[...] = dot(atm[...], edge_table(0)) + dot(grad[...], grad_edge_table())


def regrid_kernel(sources, blocks, a0, a1, a2, crossed, far, weights, atm, grad, edges, regridded, keep, give, sides, held, acc):
    tile = lax.axis_index("tile")
    facing = 1 - 2 * (tile & 1)
    for i, ref in enumerate((a0, a1, a2)):
        held[96 * i : 96 * i + 96, :] = ref[0:96, :]
    held[288:576, :] = crossed[0:288, :]
    held[576:672, :] = far[...]
    acc[...] = jnp.zeros_like(acc)
    for k in range(4):
        shift = ((sources[0, k] - tile - HALF + 3 + 2 * TILES) & (TILES - 1)) - 3
        odd = shift & 1
        even_at = 1 - (shift >> 1)
        odd_at = jnp.where(shift == -3 * facing, 6, 4 + ((facing - shift) >> 1))
        at = jnp.clip(jnp.where(odd == 1, odd_at, even_at), 0, 6)
        for slot in range(3):
            block = blocks[0, 3 * k + slot]

            @pl.when(block >= 0)
            def _():
                rows = pl.ds(pl.multiple_of(at * 96 + 32 * slot, 32), 32)
                into = pl.ds(pl.multiple_of(block * 32, 32), 32)
                acc[into, :] += dot(held[rows, :], weights[3 * k + slot])

    for a in range(8):
        regridded[:, LANES * a : LANES * (a + 1)] = acc[32 * a : 32 * (a + 1), :].astype(BF)

    def north(out):
        out[:, 0:256] = atm[:, 0:256]
        out[:, 256:384] = grad[:, 0:128]
        out[0:32, 384:512] = regridded[:, 0:128]
        out[32:64, 384:512] = regridded[:, 128:256]

    def south(out):
        out[:, 0:256] = atm[:, 768:1024]
        out[:, 256:384] = grad[:, 896:1024]
        out[0:32, 384:512] = regridded[:, 768:896]
        out[32:64, 384:512] = regridded[:, 896:1024]

    @pl.when(facing == 1)
    def _():
        south(keep)
        north(give)

    @pl.when(facing != 1)
    def _():
        north(keep)
        south(give)

    sides[0:32, :] = (edges[0:32, :] + dot(regridded[...], edge_table(64))).astype(BF)
    sides[32:64, :] = edges[32:64, :].astype(BF)


def select_kernel(own_near, mate_near, gathered, bias, own, mate):
    core = lax.axis_index("tile") & 1
    for near, out in ((own_near, own), (mate_near, mate)):

        def strip(direction):
            device = near[0, direction]
            side = 1 if direction in (1, 6, 7) else 0
            here = (device >= 0) & (core == side)
            first = pl.multiple_of(jnp.where(here, (device & 1) ^ side, 0) * 512, 512)
            data = gathered[jnp.where(here, (device & 7) >> 1, 0), :, pl.ds(first, 512)]
            return jnp.where(here, data, jnp.zeros_like(data))

        def beside(direction):
            device = near[0, direction]
            here = (device >= 0) & ((device & 1) == core)
            data = gathered[jnp.where(here, (device & 7) >> 1, 0), :, 1024:1152]
            return jnp.where(here, data, jnp.zeros_like(data))

        out[:, 0:512] = strip(0)
        out[:, 512:1024] = strip(1)
        total = jnp.zeros((64, 128), F32)
        halves = [jnp.zeros((32, 128), F32), jnp.zeros((32, 128), F32)]
        for east in (0, 1):
            data = beside(2 + east)
            given = 0 if east else 16
            picks = beside_table(given, 8 + 2 * east, 4) + beside_grad_table(32 if east else 40, OG0 + 2 + east)
            total = total + dot(data, picks)
            halves[east] = halves[east] + dot(data[0:32], beside_table(64 + given, OC0 + 4, 2))
            col = 0 if east else 126
            for at_south in (0, 1):
                first, beyond = (10, 9) if at_south else (0, 0)
                data = strip(4 + 2 * at_south + east)
                for q in (0, 1):
                    total = total + dot(data[:, 128 * q : 128 * q + 128], pair_table(col, 4 * (first + q) + 2 * east))
                    halves[east] = halves[east] + dot(data[32 * q : 32 * q + 32, 384:512], pair_table(col, OC0 + 2 * (first + q)))
                total = total + dot(data[:, 256:384], single_table(0 if east else 127, OG0 + 2 * beyond + east))
        out[0:32, 1024:1152] = (total[0:32] + halves[0]).astype(BF)
        out[32:64, 1024:1152] = (total[32:64] + halves[1]).astype(BF)
    side = own[:, 1024:1152].astype(F32)
    row, _ = grid(64, 64)
    _, lane = grid(64, 128)
    rest = jnp.sum(jnp.where(row == lane[:, 0:64], bias[...], 0.0), axis=1, keepdims=True)
    for i in range(3):
        part = rest.astype(BF).astype(F32)
        side = jnp.where(lane == BIAS0 + i, part, side)
        rest = rest - part
    own[:, 1024:1152] = side.astype(BF)


def forward_kernel(
    inner, outer_held, flipped, output, z_all, mine, theirs, side_atm, taps, side_taps, grads, outs, weights, outer, lifted, sems
):
    chan, core = lax.axis_index("chan"), lax.axis_index("tile") & 1
    fetches = [pltpu.make_async_copy(outer_held, outer, sems.at[0])]
    for c in range(4):
        own = slice(64 * c, 64 * c + 64)
        state = taps.at[pl.ds(384 + 64 * c, 64), pl.ds(256, 1024)]
        fetches.append(pltpu.make_async_copy(inner.at[c, pl.ds(0, 64)], state, sems.at[1 + c]))
        fetches.append(pltpu.make_async_copy(inner.at[c, pl.ds(64, 64)], grads.at[own, pl.ds(128, 1024)], sems.at[5 + c]))
        sea = taps.at[pl.ds(640 + 32 * c, 32), pl.ds(256, 1024)]
        fetches.append(pltpu.make_async_copy(inner.at[c, pl.ds(128, 32)], sea, sems.at[9 + c]))
    fetches.append(pltpu.make_async_copy(flipped, weights, sems.at[13]))
    for fetch in fetches:
        fetch.start()
    fetches[0].wait()
    _, lane = grid(64, 128)
    for c in range(4):
        atm = slice(64 * c, 64 * c + 64)
        mid = slice(384 + 64 * c, 448 + 64 * c)
        sea = slice(640 + 32 * c, 672 + 32 * c)
        taps[mid, 0:256] = outer[c, :, 0:256]
        taps[mid, 1280:1536] = outer[c, :, 512:768]
        side_atm[atm, :] = outer[c, :, 1024:1152]
        taps[sea, 0:128] = outer[c, 0:32, 384:512]
        taps[sea, 128:256] = outer[c, 32:64, 384:512]
        taps[sea, 1280:1408] = outer[c, 0:32, 896:1024]
        taps[sea, 1408:1536] = outer[c, 32:64, 896:1024]
        side = dot(outer[c, 0:32, 1024:1152], ocean_side_table(0)) + dot(outer[c, 32:64, 1024:1152], ocean_side_table(1))
        side_atm[256 + 32 * c : 288 + 32 * c, :] = side.astype(BF)
        grads[atm, 0:128] = outer[c, :, 256:384]
        grads[atm, 1152:1280] = outer[c, :, 768:896]
        side = outer[c, :, 1024:1152]
        grads[atm, 1280:1408] = jnp.where((lane >= OG0) & (lane < OC0), side, jnp.zeros_like(side))
    for fetch in fetches[1:13]:
        fetch.wait()
    side = side_atm[...]
    shifts, edges = shift_tables(), edge_rows()
    for r in range(12):
        lanes = slice(128 * r, 128 * r + 128)
        table = jnp.concatenate([shifts, edge_marks(edges, 4 * r + 1)], axis=0)
        moved = dot(jnp.concatenate([taps[384:768, lanes], side], axis=1), table).astype(BF)
        taps[0:384, lanes] = moved[:, 0:128]
        taps[768:1152, lanes] = moved[:, 128:256]
    _, lane = grid(384, 128)
    columns = dot(taps[384:768, :], gather_table()).astype(BF)
    columns = jnp.where(lane < 48, side, columns)
    moved = dot(columns, jnp.concatenate([tap_table(s, t) for s in (-1, 0, 1) for t in (-1, 0, 1)], axis=1)).astype(BF)
    for s in range(3):
        for t in range(3):
            at = 128 * (3 * s + t)
            side_taps[384 * t : 384 * t + 384, 128 * s : 128 * s + 128] = moved[:, at : at + 128]
    bias = jnp.concatenate(
        [jnp.sum(outer[c, :, 1024 + BIAS0 : 1024 + BIAS0 + 3].astype(F32), axis=1, keepdims=True) for c in range(4)], axis=0
    )

    fetches[13].wait()

    def activate(total, lanes):
        pre = total + bias
        gate = 1.0 / (1.0 + jnp.exp(-pre))
        z_all[:, lanes] = (grads[:, lanes].astype(F32) * gate * (1.0 + pre * (1.0 - gate))).astype(BF)
        return pre * gate

    for r in range(0, 10, 2):
        total = jnp.zeros((256, 256), F32)
        for s in range(3):
            total = total + dot(weights[s], taps[:, 128 * (r + s) : 128 * (r + s) + 256])
        silu = activate(total, slice(128 * r, 128 * r + 256))
        for q in (0, 1):
            row = r + q - 1
            if 0 <= row < 8:
                state = taps[384:640, 128 * (row + 2) : 128 * (row + 3)].astype(F32)
                outs[:, 128 * row : 128 * row + 128] = (state + silu[:, 128 * q : 128 * q + 128]).astype(BF)
    total = jnp.zeros((256, 128), F32)
    for s in range(3):
        total = total + dot(weights[s], side_taps[:, 128 * s : 128 * s + 128])
    activate(total, slice(1280, 1408))
    rows = pl.ds(pl.multiple_of(chan * 64, 64), 64)
    output[...] = outs[rows, :]
    own = z_all[rows, 128:1152]
    sums = dot_last(jnp.ones((16, 1024), BF), own)
    for half, first in ((0, mine), (1, theirs)):
        first[54:64] = jnp.zeros((10, 16, 128), first.dtype)
        first[54, :, 0:64] = sums.astype(first.dtype)
    lifted[...] = jnp.zeros_like(lifted)
    for s in range(3):
        lifted[64 * s : 64 * s + 64, 128 * (s + 1) : 128 * (s + 1) + 1024] = own
    found = dot_last(lifted[...], taps[...])
    for s in range(3):
        for t in range(3):
            for a in range(4):
                for l in range(3):
                    piece = found[64 * s + 16 * a : 64 * s + 16 * a + 16, 384 * t + 128 * l : 384 * t + 128 * l + 128]
                    row = 4 * (3 * s + t) + a
                    half, at = row // 18, (row % 18) * 3 + l

                    @pl.when(core == half)
                    def _():
                        mine[at] = piece

                    @pl.when(core != half)
                    def _():
                        theirs[at] = piece.astype(BF)


def backward_kernel(
    sources, blocks, z_all, weights_held, regrid_held, grad_held,
    input_grad, r0, r1, r2, far, taps, delta, terms, weights, regrid_weights, grad, sems,
):
    pairs = ((weights_held, weights), (grad_held, grad), (regrid_held, regrid_weights))
    fetches = [pltpu.make_async_copy(held, ref, sems.at[i]) for i, (held, ref) in enumerate(pairs)]
    for fetch in fetches:
        fetch.start()
    tile, chan = lax.axis_index("tile"), lax.axis_index("chan")
    facing = 1 - 2 * (tile & 1)
    side = z_all[:, 1280:1408]
    shifts, edges = shift_tables(), edge_rows()
    for r in range(10):
        lanes = slice(128 * r, 128 * r + 128)
        table = jnp.concatenate([shifts, edge_marks(edges, OG0 + 2 * r)], axis=0)
        moved = dot(jnp.concatenate([z_all[:, lanes], side], axis=1), table).astype(BF)
        taps[512:768, lanes] = moved[:, 0:128]
        taps[0:256, lanes] = moved[:, 128:256]
    taps[256:512, :] = z_all[:, 0:1280]
    atm_rows = pl.ds(pl.multiple_of(chan * 64, 64), 64)
    sea_rows = pl.ds(pl.multiple_of(256 + chan * 32, 32), 32)
    for fetch in fetches:
        fetch.wait()
    for q in range(4):
        atm_total = jnp.zeros((64, 256), F32)
        sea_total = jnp.zeros((32, 256), F32)
        for s in range(3):
            first = 128 * (2 * q + 2 - s)
            for t in range(3):
                window = taps[256 * t : 256 * t + 256, first : first + 256]
                atm_total = atm_total + dot(weights[3 * s + t, atm_rows, :], window)
                sea_total = sea_total + dot(weights[3 * s + t, sea_rows, :], window)
        lanes = slice(256 * q, 256 * q + 256)
        input_grad[:, lanes] = (grad[:, lanes].astype(F32) + atm_total).astype(BF)
        delta[:, lanes] = sea_total.astype(BF)
    for e in range(12):
        block = blocks[0, e]
        lanes = pl.ds(pl.multiple_of(jnp.maximum(block, 0) * LANES, LANES), LANES)
        term = dot_last(delta[:, lanes], regrid_weights[e])
        terms[32 * e : 32 * e + 32, :] = jnp.where(block >= 0, term, 0.0).astype(BF)
    terms[384:480, :] = jnp.zeros((96, 128), BF)

    def parcel(out, at, shift):
        target = (tile + HALF + shift) & (TILES - 1)
        found = jnp.int32(4)
        for k in range(4):
            found = jnp.where(sources[0, k] == target, k, found)
        out[at : at + 96, :] = terms[pl.ds(pl.multiple_of(found * 96, 96), 96), :]

    for step, out in zip(CHIP_STEPS, (r0, r1, r2)):
        parcel(out, 0, 2 * step)
        parcel(out, 96, 2 * step + facing)
    parcel(far, 0, -3 * facing)


def return_kernel(sends, a0, a1, a2, crossed, far, ocean_grad, acc):
    tile = lax.axis_index("tile")
    facing = 1 - 2 * (tile & 1)
    acc[...] = jnp.zeros_like(acc)

    def add(ref, first, shift):
        sender = (tile + HALF + shift) & (TILES - 1)
        for slot in range(3):
            block = sends[slot, 0, sender]

            @pl.when(block >= 0)
            def _():
                into = pl.ds(pl.multiple_of(block * 32, 32), 32)
                acc[into, :] += ref[first + 32 * slot : first + 32 * slot + 32, :].astype(F32)

    for i, (step, ref) in enumerate(zip(CHIP_STEPS, (a0, a1, a2))):
        add(ref, 0, -2 * step)
        add(crossed, 96 * i, -2 * step + facing)
    add(far, 0, -3 * facing)
    for b in range(8):
        ocean_grad[:, LANES * b : LANES * (b + 1)] = acc[32 * b : 32 * (b + 1), :]


def add_kernel(mine, crossed, total):
    total[...] = (mine[...] + crossed[...].astype(F32)).astype(BF)


def sum_kernel(scale, arrived, out):
    total = (jnp.sum(arrived[...].astype(F32), axis=0) * scale).astype(BF)
    for i in range(64):
        out[i] = total


def finish_kernel(held, crossed, weight_grad):
    core = lax.axis_index("tile") & 1
    for half in range(2):
        for a in range(18):
            row = 18 * half + a
            k, part = row // 4, row % 4
            for l in range(3):
                at = 3 * a + l
                piece = jnp.where(core == half, held[at].astype(F32), crossed[at].astype(F32))
                weight_grad[k, 16 * part : 16 * part + 16, 128 * l : 128 * l + 128] = piece


def send(array, target):
    return lax.ppermute(array, "tile", [(i, target(i)) for i in range(TILES)])


def chip_send(array, at):
    return send(array, lambda i: (i + HALF + 2 * CHIP_STEPS[at]) % TILES)


def far_send(array):
    return send(array, lambda i: (i + HALF - 3 * (1 - 2 * (i % 2))) % TILES)


def to_mate(array):
    return send(array, lambda i: i ^ 1)


def on_device(
    atm_state,
    ocean_state,
    conv_weight,
    conv_bias,
    regrid_weight,
    out_grad,
    atm_neighbours,
    coupling_sources,
    coupling_blocks,
    coupling_sends,
):
    sends = jnp.transpose(coupling_sends, (2, 0, 1))
    b0, b1, b2, far = call(parcels_kernel, [((192, 128), BF)] * 3 + [((96, 128), BF)], [SMEM, VMEM])(sends, ocean_state)
    a0, a1, a2, far = chip_send(b0, 0), chip_send(b1, 1), chip_send(b2, 2), far_send(far)
    flipped = jnp.swapaxes(conv_weight.reshape(3, 1152, 256), 1, 2)
    a0, a1, a2, far, flipped = lax.optimization_barrier((a0, a1, a2, far, flipped))
    table = jnp.pad(atm_neighbours.astype(BF), ((0, 15), (0, 120)))
    crossed = to_mate(jnp.concatenate([a0[96:], a1[96:], a2[96:], table], axis=0))
    mate_near = crossed[288:289, 0:8].astype(jnp.int32)
    (edges,) = call(edges_kernel, [((64, 128), F32)], [VMEM, VMEM])(atm_state, out_grad)
    regridded, keep, give, sides = call(
        regrid_kernel,
        [((32, 1024), BF), ((64, 512), BF), ((64, 512), BF), ((64, 128), BF)],
        [SMEM] * 2 + [VMEM] * 9,
        [pltpu.VMEM((672, 128), BF), pltpu.VMEM((256, 128), F32)],
    )(coupling_sources, coupling_blocks, a0, a1, a2, crossed, far, regrid_weight, atm_state, out_grad, edges)
    got, atm_now, grad_now = lax.optimization_barrier((to_mate(give), atm_state, out_grad))
    (copies,) = call(copies_kernel, [((4, 160, 1024), BF)], [VMEM] * 3)(atm_now, grad_now, regridded)
    inner = lax.all_to_all(copies, "chan", 0, 0)
    pair = jnp.concatenate([keep, got], axis=1)
    pairs = [(i, i + 8 - 16 * (i % 2)) for i in range(TILES)]
    arrived = lax.ppermute(pair, "tile", [(i, j) for i, j in pairs if 0 <= j < TILES])
    strips = jnp.concatenate([arrived, sides], axis=1)
    strips = lax.all_gather(strips, "tile", axis_index_groups=ROW_CHIPS)
    own, mate = call(select_kernel, [((64, 1152), BF)] * 2, [SMEM] * 2 + [VMEM] * 2, cost=12)(
        atm_neighbours, mate_near, strips, conv_bias.reshape(1, 64)
    )
    shard = own + to_mate(mate)
    shard, inner = lax.optimization_barrier((shard, inner))
    outer = lax.all_gather(shard, "chan")
    atm_output, z_all, mine, theirs = call(
        forward_kernel,
        [((64, 1024), BF), ((256, 1408), BF), ((64, 16, 128), F32), ((64, 16, 128), BF)],
        [HELD] * 3,
        [
            pltpu.VMEM((384, 128), BF),
            pltpu.VMEM((1152, 1536), BF),
            pltpu.VMEM((1152, 384), BF),
            pltpu.VMEM((256, 1408), BF),
            pltpu.VMEM((256, 1024), BF),
            pltpu.VMEM((3, 256, 1152), BF),
            pltpu.VMEM((4, 64, 1152), BF),
            pltpu.VMEM((192, 1536), BF),
            pltpu.SemaphoreType.DMA((14,)),
        ],
        limit=56,
        cost=10,
    )(inner, outer, flipped)
    (total,) = call(add_kernel, [((64, 16, 128), BF)], [VMEM, VMEM])(mine, to_mate(theirs))
    total, z_all = lax.optimization_barrier((total, z_all))
    shares = lax.all_to_all(total, "tile", 0, 0, axis_index_groups=SAME_CORE)
    input_grad, b0, b1, b2, far = call(
        backward_kernel,
        [((64, 1024), BF)] + [((192, 128), BF)] * 3 + [((96, 128), BF)],
        [SMEM] * 2 + [VMEM] + [HELD] * 3,
        [
            pltpu.VMEM((768, 1280), BF),
            pltpu.VMEM((32, 1024), BF),
            pltpu.VMEM((480, 128), BF),
            pltpu.VMEM((9, 384, 256), BF),
            pltpu.VMEM((12, 128, 128), BF),
            pltpu.VMEM((64, 1024), BF),
            pltpu.SemaphoreType.DMA((3,)),
        ],
        limit=48,
        cost=4,
    )(coupling_sources, coupling_blocks, z_all, conv_weight, regrid_weight, out_grad)
    a0, a1, a2 = chip_send(b0, 0), chip_send(b1, 1), chip_send(b2, 2)
    shares, a0, a1, far = lax.optimization_barrier((shares, a0, a1, far))
    scale = 1.0 / math.sqrt(atm_state.shape[1] * TILES)
    (summed,) = call(functools.partial(sum_kernel, scale), [((64, 16, 128), BF)], [VMEM])(shares)
    summed, far = lax.optimization_barrier((summed, far))
    held = lax.all_to_all(summed, "tile", 0, 0, axis_index_groups=SAME_CORE)
    far = far_send(far)
    a2, far = lax.optimization_barrier((a2, far))
    crossed = to_mate(jnp.concatenate([a0[96:], a1[96:], a2[96:]], axis=0))
    (ocean_grad,) = call(return_kernel, [((32, 1024), F32)], [SMEM] + [VMEM] * 5, [pltpu.VMEM((256, 128), F32)])(
        sends, a0, a1, a2, crossed, far
    )
    held, ocean_grad = lax.optimization_barrier((held, ocean_grad))
    crossed = to_mate(held)
    bias_grad = held[54, 0, 0:64].astype(F32)
    (weight_grad,) = call(finish_kernel, [((9, 64, 384), F32)], [VMEM, VMEM])(held, crossed)
    return atm_output, input_grad, ocean_grad, jnp.swapaxes(weight_grad, 1, 2), bias_grad


def solution(mesh):
    placed = (
        P("chan", "tile"),
        P("chan", "tile"),
        P(),
        P("chan"),
        P("tile", None, None),
        P("chan", "tile"),
        P("tile", None),
        P("tile", None),
        P("tile", None),
        P("tile", None, None),
    )
    return jax.shard_map(
        on_device,
        mesh=mesh,
        in_specs=placed,
        out_specs=(
            P("chan", "tile"),
            P("chan", "tile"),
            P("chan", "tile"),
            P(None, None, "chan"),
            P("chan"),
        ),
        check_vma=False,
    )
```

```python
import functools
import math

import jax
import jax.numpy as jnp
from jax import lax
from jax.experimental import pallas as pl
from jax.experimental.pallas import tpu as pltpu
from jax.sharding import PartitionSpec as P

BF, F32 = jnp.bfloat16, jnp.float32
TILES = 128
HALF = TILES // 2
LANES = 128
OG0, OC0, BIAS0 = 48, 68, 92
VMEM = pl.BlockSpec(memory_space=pltpu.VMEM)
SMEM = pl.BlockSpec(memory_space=pltpu.SMEM)
HELD = pl.BlockSpec(memory_space=pl.ANY)

CHIP_STEPS = (-1, 0, 1)
ROW_CHIPS = [[8 * r + 2 * i + c for i in range(4)] for r in range(16) for c in range(2)]
SAME_CORE = [[2 * i + c for i in range(64)] for c in range(2)]


def grid(rows, columns):
    shape = (rows, columns)
    return lax.broadcasted_iota(jnp.int32, shape, 0), lax.broadcasted_iota(jnp.int32, shape, 1)


def marks(where):
    return jnp.where(where, 1.0, 0.0).astype(BF)


def edge_table(first):
    cell, lane = grid(1024, 128)
    col, at = cell & 127, first + 2 * (cell >> 7)
    return marks(((col < 2) & (lane == at + col)) | ((col >= 126) & (lane == at + col - 110)))


def grad_edge_table():
    cell, lane = grid(1024, 128)
    col, row = cell & 127, cell >> 7
    return marks(((col == 0) & (lane == 32 + row)) | ((col == 127) & (lane == 40 + row)))


def pair_table(given, to):
    lane, into = grid(128, 128)
    return marks((lane >= given) & (lane < given + 2) & (into - to == lane - given))


def single_table(given, to):
    lane, into = grid(128, 128)
    return marks((lane == given) & (into == to))


def beside_table(given, to, step):
    lane, into = grid(128, 128)
    at = lane - given
    return marks((at >= 0) & (at < 16) & (into == to + step * (at >> 1) + (at & 1)))


def beside_grad_table(given, to):
    lane, into = grid(128, 128)
    at = lane - given
    return marks((at >= 0) & (at < 8) & (into == to + 2 * at))


def shift_table(step):
    lane, into = grid(128, 128)
    return marks(lane == into + step)


def shift_tables():
    return jnp.concatenate([shift_table(-1), shift_table(1)], axis=1)


def edge_rows():
    lane, into = grid(128, 256)
    return jnp.where(into == 0, lane, jnp.where(into == 255, lane - 1, -8))


def edge_marks(rows, first):
    return marks(rows == first)


def gather_table():
    lane, into = grid(1536, 128)
    col, row = lane & 127, lane >> 7
    return marks(((col == 0) & (into == 48 + 2 * row)) | ((col == 127) & (into == 49 + 2 * row)))


def tap_table(s, t):
    lane, into = grid(128, 128)
    at = into - OG0
    east, row = at & 1, (at >> 1) + s + 1
    col = jnp.where(east == 1, 128, -1) + t
    near = jnp.where(col == 0, 48 + 2 * row, 49 + 2 * row)
    far = jnp.where(col < 0, 4 * row + col + 2, 4 * row + col - 126)
    given = jnp.where((col == 0) | (col == 127), near, far)
    return marks((at >= 0) & (at < 20) & (lane == given))


def ocean_side_table(east):
    lane, into = grid(128, 128)
    at = lane - OC0
    return marks((at >= 0) & (at < 24) & (into == 4 * (at >> 1) + (at & 1) + 2 * east))


def dot(a, b):
    return jnp.dot(a, b, preferred_element_type=F32)


def dot_last(a, b):
    return lax.dot_general(a, b, (((1,), (1,)), ((), ())), preferred_element_type=F32)


def call(kernel, outs, in_specs, scratch=(), limit=32, cost=1):
    return pl.pallas_call(
        kernel,
        out_shape=[jax.ShapeDtypeStruct(shape, dtype) for shape, dtype in outs],
        in_specs=list(in_specs),
        out_specs=[VMEM] * len(outs),
        scratch_shapes=list(scratch),
        compiler_params=pltpu.CompilerParams(vmem_limit_bytes=limit << 20),
        cost_estimate=pl.CostEstimate(flops=cost * 10**9, bytes_accessed=cost * 3 * 10**6, transcendentals=0),
    )


def parcels_kernel(sends, ocean, *outs):
    tile = lax.axis_index("tile")
    facing = 1 - 2 * (tile & 1)

    def parcel(out, at, shift):
        target = (tile + HALF + shift) & (TILES - 1)
        for slot in range(3):
            block = sends[slot, 0, target]
            start = pl.multiple_of(jnp.maximum(block, 0) * LANES, LANES)
            data = ocean[:, pl.ds(start, LANES)]
            out[at + 32 * slot : at + 32 * slot + 32, :] = jnp.where(block >= 0, data, jnp.zeros_like(data))

    for step, out in zip(CHIP_STEPS, outs):
        parcel(out, 0, 2 * step)
        parcel(out, 96, 2 * step + facing)
    parcel(outs[3], 0, -3 * facing)


def copies_kernel(atm, grad, regridded, copies):
    for chan in range(4):
        copies[chan, 0:64] = atm[...]
        copies[chan, 64:128] = grad[...]
        copies[chan, 128:160] = regridded[...]


def edges_kernel(atm, grad, edges):
    edges[...] = dot(atm[...], edge_table(0)) + dot(grad[...], grad_edge_table())


def regrid_kernel(sources, blocks, a0, a1, a2, crossed, far, weights, atm, grad, edges, regridded, keep, give, sides, held, acc):
    tile = lax.axis_index("tile")
    facing = 1 - 2 * (tile & 1)
    for i, ref in enumerate((a0, a1, a2)):
        held[96 * i : 96 * i + 96, :] = ref[0:96, :]
    held[288:576, :] = crossed[0:288, :]
    held[576:672, :] = far[...]
    acc[...] = jnp.zeros_like(acc)
    for k in range(4):
        shift = ((sources[0, k] - tile - HALF + 3 + 2 * TILES) & (TILES - 1)) - 3
        odd = shift & 1
        even_at = 1 - (shift >> 1)
        odd_at = jnp.where(shift == -3 * facing, 6, 4 + ((facing - shift) >> 1))
        at = jnp.clip(jnp.where(odd == 1, odd_at, even_at), 0, 6)
        for slot in range(3):
            block = blocks[0, 3 * k + slot]

            @pl.when(block >= 0)
            def _():
                rows = pl.ds(pl.multiple_of(at * 96 + 32 * slot, 32), 32)
                into = pl.ds(pl.multiple_of(block * 32, 32), 32)
                acc[into, :] += dot(held[rows, :], weights[3 * k + slot])

    for a in range(8):
        regridded[:, LANES * a : LANES * (a + 1)] = acc[32 * a : 32 * (a + 1), :].astype(BF)

    def north(out):
        out[:, 0:256] = atm[:, 0:256]
        out[:, 256:384] = grad[:, 0:128]
        out[0:32, 384:512] = regridded[:, 0:128]
        out[32:64, 384:512] = regridded[:, 128:256]

    def south(out):
        out[:, 0:256] = atm[:, 768:1024]
        out[:, 256:384] = grad[:, 896:1024]
        out[0:32, 384:512] = regridded[:, 768:896]
        out[32:64, 384:512] = regridded[:, 896:1024]

    @pl.when(facing == 1)
    def _():
        south(keep)
        north(give)

    @pl.when(facing != 1)
    def _():
        north(keep)
        south(give)

    sides[0:32, :] = (edges[0:32, :] + dot(regridded[...], edge_table(64))).astype(BF)
    sides[32:64, :] = edges[32:64, :].astype(BF)


def select_kernel(own_near, mate_near, gathered, bias, own, mate):
    core = lax.axis_index("tile") & 1
    for near, out in ((own_near, own), (mate_near, mate)):

        def strip(direction):
            device = near[0, direction]
            side = 1 if direction in (1, 6, 7) else 0
            here = (device >= 0) & (core == side)
            first = pl.multiple_of(jnp.where(here, (device & 1) ^ side, 0) * 512, 512)
            data = gathered[jnp.where(here, (device & 7) >> 1, 0), :, pl.ds(first, 512)]
            return jnp.where(here, data, jnp.zeros_like(data))

        def beside(direction):
            device = near[0, direction]
            here = (device >= 0) & ((device & 1) == core)
            data = gathered[jnp.where(here, (device & 7) >> 1, 0), :, 1024:1152]
            return jnp.where(here, data, jnp.zeros_like(data))

        out[:, 0:512] = strip(0)
        out[:, 512:1024] = strip(1)
        total = jnp.zeros((64, 128), F32)
        halves = [jnp.zeros((32, 128), F32), jnp.zeros((32, 128), F32)]
        for east in (0, 1):
            data = beside(2 + east)
            given = 0 if east else 16
            picks = beside_table(given, 8 + 2 * east, 4) + beside_grad_table(32 if east else 40, OG0 + 2 + east)
            total = total + dot(data, picks)
            halves[east] = halves[east] + dot(data[0:32], beside_table(64 + given, OC0 + 4, 2))
            col = 0 if east else 126
            for at_south in (0, 1):
                first, beyond = (10, 9) if at_south else (0, 0)
                data = strip(4 + 2 * at_south + east)
                for q in (0, 1):
                    total = total + dot(data[:, 128 * q : 128 * q + 128], pair_table(col, 4 * (first + q) + 2 * east))
                    halves[east] = halves[east] + dot(data[32 * q : 32 * q + 32, 384:512], pair_table(col, OC0 + 2 * (first + q)))
                total = total + dot(data[:, 256:384], single_table(0 if east else 127, OG0 + 2 * beyond + east))
        out[0:32, 1024:1152] = (total[0:32] + halves[0]).astype(BF)
        out[32:64, 1024:1152] = (total[32:64] + halves[1]).astype(BF)
    side = own[:, 1024:1152].astype(F32)
    row, _ = grid(64, 64)
    _, lane = grid(64, 128)
    rest = jnp.sum(jnp.where(row == lane[:, 0:64], bias[...], 0.0), axis=1, keepdims=True)
    for i in range(3):
        part = rest.astype(BF).astype(F32)
        side = jnp.where(lane == BIAS0 + i, part, side)
        rest = rest - part
    own[:, 1024:1152] = side.astype(BF)


def forward_kernel(
    inner, outer_held, flipped, output, z_all, mine, theirs, side_atm, taps, side_taps, grads, outs, weights, outer, lifted, sems
):
    chan, core = lax.axis_index("chan"), lax.axis_index("tile") & 1
    fetches = [pltpu.make_async_copy(outer_held, outer, sems.at[0])]
    for c in range(4):
        own = slice(64 * c, 64 * c + 64)
        state = taps.at[pl.ds(384 + 64 * c, 64), pl.ds(256, 1024)]
        fetches.append(pltpu.make_async_copy(inner.at[c, pl.ds(0, 64)], state, sems.at[1 + c]))
        fetches.append(pltpu.make_async_copy(inner.at[c, pl.ds(64, 64)], grads.at[own, pl.ds(128, 1024)], sems.at[5 + c]))
        sea = taps.at[pl.ds(640 + 32 * c, 32), pl.ds(256, 1024)]
        fetches.append(pltpu.make_async_copy(inner.at[c, pl.ds(128, 32)], sea, sems.at[9 + c]))
    fetches.append(pltpu.make_async_copy(flipped, weights, sems.at[13]))
    for fetch in fetches:
        fetch.start()
    fetches[0].wait()
    _, lane = grid(64, 128)
    for c in range(4):
        atm = slice(64 * c, 64 * c + 64)
        mid = slice(384 + 64 * c, 448 + 64 * c)
        sea = slice(640 + 32 * c, 672 + 32 * c)
        taps[mid, 0:256] = outer[c, :, 0:256]
        taps[mid, 1280:1536] = outer[c, :, 512:768]
        side_atm[atm, :] = outer[c, :, 1024:1152]
        taps[sea, 0:128] = outer[c, 0:32, 384:512]
        taps[sea, 128:256] = outer[c, 32:64, 384:512]
        taps[sea, 1280:1408] = outer[c, 0:32, 896:1024]
        taps[sea, 1408:1536] = outer[c, 32:64, 896:1024]
        side = dot(outer[c, 0:32, 1024:1152], ocean_side_table(0)) + dot(outer[c, 32:64, 1024:1152], ocean_side_table(1))
        side_atm[256 + 32 * c : 288 + 32 * c, :] = side.astype(BF)
        grads[atm, 0:128] = outer[c, :, 256:384]
        grads[atm, 1152:1280] = outer[c, :, 768:896]
        side = outer[c, :, 1024:1152]
        grads[atm, 1280:1408] = jnp.where((lane >= OG0) & (lane < OC0), side, jnp.zeros_like(side))
    for fetch in fetches[1:13]:
        fetch.wait()
    side = side_atm[...]
    shifts, edges = shift_tables(), edge_rows()
    for r in range(12):
        lanes = slice(128 * r, 128 * r + 128)
        table = jnp.concatenate([shifts, edge_marks(edges, 4 * r + 1)], axis=0)
        moved = dot(jnp.concatenate([taps[384:768, lanes], side], axis=1), table).astype(BF)
        taps[0:384, lanes] = moved[:, 0:128]
        taps[768:1152, lanes] = moved[:, 128:256]
    _, lane = grid(384, 128)
    columns = dot(taps[384:768, :], gather_table()).astype(BF)
    columns = jnp.where(lane < 48, side, columns)
    moved = dot(columns, jnp.concatenate([tap_table(s, t) for s in (-1, 0, 1) for t in (-1, 0, 1)], axis=1)).astype(BF)
    for s in range(3):
        for t in range(3):
            at = 128 * (3 * s + t)
            side_taps[384 * t : 384 * t + 384, 128 * s : 128 * s + 128] = moved[:, at : at + 128]
    bias = jnp.concatenate(
        [jnp.sum(outer[c, :, 1024 + BIAS0 : 1024 + BIAS0 + 3].astype(F32), axis=1, keepdims=True) for c in range(4)], axis=0
    )

    fetches[13].wait()

    def activate(total, lanes):
        pre = total + bias
        gate = 1.0 / (1.0 + jnp.exp(-pre))
        z_all[:, lanes] = (grads[:, lanes].astype(F32) * gate * (1.0 + pre * (1.0 - gate))).astype(BF)
        return pre * gate

    for r in range(0, 10, 2):
        total = jnp.zeros((256, 256), F32)
        for s in range(3):
            total = total + dot(weights[s], taps[:, 128 * (r + s) : 128 * (r + s) + 256])
        silu = activate(total, slice(128 * r, 128 * r + 256))
        for q in (0, 1):
            row = r + q - 1
            if 0 <= row < 8:
                state = taps[384:640, 128 * (row + 2) : 128 * (row + 3)].astype(F32)
                outs[:, 128 * row : 128 * row + 128] = (state + silu[:, 128 * q : 128 * q + 128]).astype(BF)
    total = jnp.zeros((256, 128), F32)
    for s in range(3):
        total = total + dot(weights[s], side_taps[:, 128 * s : 128 * s + 128])
    activate(total, slice(1280, 1408))
    rows = pl.ds(pl.multiple_of(chan * 64, 64), 64)
    output[...] = outs[rows, :]
    own = z_all[rows, 128:1152]
    sums = dot_last(jnp.ones((16, 1024), BF), own)
    for half, first in ((0, mine), (1, theirs)):
        first[54:64] = jnp.zeros((10, 16, 128), first.dtype)
        first[54, :, 0:64] = sums.astype(first.dtype)
    lifted[...] = jnp.zeros_like(lifted)
    for s in range(3):
        lifted[64 * s : 64 * s + 64, 128 * (s + 1) : 128 * (s + 1) + 1024] = own
    found = dot_last(lifted[...], taps[...])
    for s in range(3):
        for t in range(3):
            for a in range(4):
                for l in range(3):
                    piece = found[64 * s + 16 * a : 64 * s + 16 * a + 16, 384 * t + 128 * l : 384 * t + 128 * l + 128]
                    row = 4 * (3 * s + t) + a
                    half, at = row // 18, (row % 18) * 3 + l

                    @pl.when(core == half)
                    def _():
                        mine[at] = piece.astype(BF)

                    @pl.when(core != half)
                    def _():
                        theirs[at] = piece.astype(BF)


def backward_kernel(
    sources, blocks, z_all, weights_held, regrid_held, grad_held,
    input_grad, r0, r1, r2, far, taps, delta, terms, weights, regrid_weights, grad, sems,
):
    pairs = ((weights_held, weights), (grad_held, grad), (regrid_held, regrid_weights))
    fetches = [pltpu.make_async_copy(held, ref, sems.at[i]) for i, (held, ref) in enumerate(pairs)]
    for fetch in fetches:
        fetch.start()
    tile, chan = lax.axis_index("tile"), lax.axis_index("chan")
    facing = 1 - 2 * (tile & 1)
    side = z_all[:, 1280:1408]
    shifts, edges = shift_tables(), edge_rows()
    for r in range(10):
        lanes = slice(128 * r, 128 * r + 128)
        table = jnp.concatenate([shifts, edge_marks(edges, OG0 + 2 * r)], axis=0)
        moved = dot(jnp.concatenate([z_all[:, lanes], side], axis=1), table).astype(BF)
        taps[512:768, lanes] = moved[:, 0:128]
        taps[0:256, lanes] = moved[:, 128:256]
    taps[256:512, :] = z_all[:, 0:1280]
    atm_rows = pl.ds(pl.multiple_of(chan * 64, 64), 64)
    sea_rows = pl.ds(pl.multiple_of(256 + chan * 32, 32), 32)
    for fetch in fetches:
        fetch.wait()
    for q in range(4):
        atm_total = jnp.zeros((64, 256), F32)
        sea_total = jnp.zeros((32, 256), F32)
        for s in range(3):
            first = 128 * (2 * q + 2 - s)
            for t in range(3):
                window = taps[256 * t : 256 * t + 256, first : first + 256]
                atm_total = atm_total + dot(weights[3 * s + t, atm_rows, :], window)
                sea_total = sea_total + dot(weights[3 * s + t, sea_rows, :], window)
        lanes = slice(256 * q, 256 * q + 256)
        input_grad[:, lanes] = (grad[:, lanes].astype(F32) + atm_total).astype(BF)
        delta[:, lanes] = sea_total.astype(BF)
    for e in range(12):
        block = blocks[0, e]
        lanes = pl.ds(pl.multiple_of(jnp.maximum(block, 0) * LANES, LANES), LANES)
        term = dot_last(delta[:, lanes], regrid_weights[e])
        terms[32 * e : 32 * e + 32, :] = jnp.where(block >= 0, term, 0.0).astype(BF)
    terms[384:480, :] = jnp.zeros((96, 128), BF)

    def parcel(out, at, shift):
        target = (tile + HALF + shift) & (TILES - 1)
        found = jnp.int32(4)
        for k in range(4):
            found = jnp.where(sources[0, k] == target, k, found)
        out[at : at + 96, :] = terms[pl.ds(pl.multiple_of(found * 96, 96), 96), :]

    for step, out in zip(CHIP_STEPS, (r0, r1, r2)):
        parcel(out, 0, 2 * step)
        parcel(out, 96, 2 * step + facing)
    parcel(far, 0, -3 * facing)


def return_kernel(sends, a0, a1, a2, crossed, far, ocean_grad, acc):
    tile = lax.axis_index("tile")
    facing = 1 - 2 * (tile & 1)
    acc[...] = jnp.zeros_like(acc)

    def add(ref, first, shift):
        sender = (tile + HALF + shift) & (TILES - 1)
        for slot in range(3):
            block = sends[slot, 0, sender]

            @pl.when(block >= 0)
            def _():
                into = pl.ds(pl.multiple_of(block * 32, 32), 32)
                acc[into, :] += ref[first + 32 * slot : first + 32 * slot + 32, :].astype(F32)

    for i, (step, ref) in enumerate(zip(CHIP_STEPS, (a0, a1, a2))):
        add(ref, 0, -2 * step)
        add(crossed, 96 * i, -2 * step + facing)
    add(far, 0, -3 * facing)
    for b in range(8):
        ocean_grad[:, LANES * b : LANES * (b + 1)] = acc[32 * b : 32 * (b + 1), :]


def add_kernel(mine, crossed, total):
    total[...] = (mine[...].astype(F32) + crossed[...].astype(F32)).astype(BF)


def sum_kernel(scale, arrived, out):
    total = (jnp.sum(arrived[...].astype(F32), axis=0) * scale).astype(BF)
    for i in range(64):
        out[i] = total


def finish_kernel(held, crossed, weight_grad):
    core = lax.axis_index("tile") & 1
    for half in range(2):
        for a in range(18):
            row = 18 * half + a
            k, part = row // 4, row % 4
            for l in range(3):
                at = 3 * a + l
                piece = jnp.where(core == half, held[at].astype(F32), crossed[at].astype(F32))
                weight_grad[k, 16 * part : 16 * part + 16, 128 * l : 128 * l + 128] = piece


def send(array, target):
    return lax.ppermute(array, "tile", [(i, target(i)) for i in range(TILES)])


def chip_send(array, at):
    return send(array, lambda i: (i + HALF + 2 * CHIP_STEPS[at]) % TILES)


def far_send(array):
    return send(array, lambda i: (i + HALF - 3 * (1 - 2 * (i % 2))) % TILES)


def to_mate(array):
    return send(array, lambda i: i ^ 1)


def on_device(
    atm_state,
    ocean_state,
    conv_weight,
    conv_bias,
    regrid_weight,
    out_grad,
    atm_neighbours,
    coupling_sources,
    coupling_blocks,
    coupling_sends,
):
    sends = jnp.transpose(coupling_sends, (2, 0, 1))
    b0, b1, b2, far = call(parcels_kernel, [((192, 128), BF)] * 3 + [((96, 128), BF)], [SMEM, VMEM])(sends, ocean_state)
    a0, a1, a2, far = chip_send(b0, 0), chip_send(b1, 1), chip_send(b2, 2), far_send(far)
    flipped = jnp.swapaxes(conv_weight.reshape(3, 1152, 256), 1, 2)
    a0, a1, a2, far, flipped = lax.optimization_barrier((a0, a1, a2, far, flipped))
    table = jnp.pad(atm_neighbours.astype(BF), ((0, 15), (0, 120)))
    crossed = to_mate(jnp.concatenate([a0[96:], a1[96:], a2[96:], table], axis=0))
    mate_near = crossed[288:289, 0:8].astype(jnp.int32)
    (edges,) = call(edges_kernel, [((64, 128), F32)], [VMEM, VMEM])(atm_state, out_grad)
    regridded, keep, give, sides = call(
        regrid_kernel,
        [((32, 1024), BF), ((64, 512), BF), ((64, 512), BF), ((64, 128), BF)],
        [SMEM] * 2 + [VMEM] * 9,
        [pltpu.VMEM((672, 128), BF), pltpu.VMEM((256, 128), F32)],
    )(coupling_sources, coupling_blocks, a0, a1, a2, crossed, far, regrid_weight, atm_state, out_grad, edges)
    got, atm_now, grad_now = lax.optimization_barrier((to_mate(give), atm_state, out_grad))
    (copies,) = call(copies_kernel, [((4, 160, 1024), BF)], [VMEM] * 3)(atm_now, grad_now, regridded)
    inner = lax.all_to_all(copies, "chan", 0, 0)
    pair = jnp.concatenate([keep, got], axis=1)
    arrived = send(pair, lambda i: (i + 8 - 16 * (i % 2)) % TILES)
    strips = jnp.concatenate([arrived, sides], axis=1)
    strips = lax.all_gather(strips, "tile", axis_index_groups=ROW_CHIPS)
    own, mate = call(select_kernel, [((64, 1152), BF)] * 2, [SMEM] * 2 + [VMEM] * 2, cost=12)(
        atm_neighbours, mate_near, strips, conv_bias.reshape(1, 64)
    )
    shard = own + to_mate(mate)
    shard, inner = lax.optimization_barrier((shard, inner))
    outer = lax.all_gather(shard, "chan")
    atm_output, z_all, mine, theirs = call(
        forward_kernel,
        [((64, 1024), BF), ((256, 1408), BF), ((64, 16, 128), BF), ((64, 16, 128), BF)],
        [HELD] * 3,
        [
            pltpu.VMEM((384, 128), BF),
            pltpu.VMEM((1152, 1536), BF),
            pltpu.VMEM((1152, 384), BF),
            pltpu.VMEM((256, 1408), BF),
            pltpu.VMEM((256, 1024), BF),
            pltpu.VMEM((3, 256, 1152), BF),
            pltpu.VMEM((4, 64, 1152), BF),
            pltpu.VMEM((192, 1536), BF),
            pltpu.SemaphoreType.DMA((14,)),
        ],
        limit=56,
        cost=10,
    )(inner, outer, flipped)
    (total,) = call(add_kernel, [((64, 16, 128), BF)], [VMEM, VMEM])(mine, to_mate(theirs))
    total, z_all = lax.optimization_barrier((total, z_all))
    shares = lax.all_to_all(total, "tile", 0, 0, axis_index_groups=SAME_CORE)
    input_grad, b0, b1, b2, far = call(
        backward_kernel,
        [((64, 1024), BF)] + [((192, 128), BF)] * 3 + [((96, 128), BF)],
        [SMEM] * 2 + [VMEM] + [HELD] * 3,
        [
            pltpu.VMEM((768, 1280), BF),
            pltpu.VMEM((32, 1024), BF),
            pltpu.VMEM((480, 128), BF),
            pltpu.VMEM((9, 384, 256), BF),
            pltpu.VMEM((12, 128, 128), BF),
            pltpu.VMEM((64, 1024), BF),
            pltpu.SemaphoreType.DMA((3,)),
        ],
        limit=48,
        cost=4,
    )(coupling_sources, coupling_blocks, z_all, conv_weight, regrid_weight, out_grad)
    a0, a1, a2 = chip_send(b0, 0), chip_send(b1, 1), chip_send(b2, 2)
    shares, a0, a1, far = lax.optimization_barrier((shares, a0, a1, far))
    scale = 1.0 / math.sqrt(atm_state.shape[1] * TILES)
    (summed,) = call(functools.partial(sum_kernel, scale), [((64, 16, 128), BF)], [VMEM])(shares)
    summed, far = lax.optimization_barrier((summed, far))
    held = lax.all_to_all(summed, "tile", 0, 0, axis_index_groups=SAME_CORE)
    far = far_send(far)
    a2, far = lax.optimization_barrier((a2, far))
    crossed = to_mate(jnp.concatenate([a0[96:], a1[96:], a2[96:]], axis=0))
    (ocean_grad,) = call(return_kernel, [((32, 1024), F32)], [SMEM] + [VMEM] * 5, [pltpu.VMEM((256, 128), F32)])(
        sends, a0, a1, a2, crossed, far
    )
    held, ocean_grad = lax.optimization_barrier((held, ocean_grad))
    crossed = to_mate(held)
    bias_grad = held[54, 0, 0:64].astype(F32)
    (weight_grad,) = call(finish_kernel, [((9, 64, 384), F32)], [VMEM, VMEM])(held, crossed)
    return atm_output, input_grad, ocean_grad, jnp.swapaxes(weight_grad, 1, 2), bias_grad


def solution(mesh):
    placed = (
        P("chan", "tile"),
        P("chan", "tile"),
        P(),
        P("chan"),
        P("tile", None, None),
        P("chan", "tile"),
        P("tile", None),
        P("tile", None),
        P("tile", None),
        P("tile", None, None),
    )
    return jax.shard_map(
        on_device,
        mesh=mesh,
        in_specs=placed,
        out_specs=(
            P("chan", "tile"),
            P("chan", "tile"),
            P("chan", "tile"),
            P(None, None, "chan"),
            P("chan"),
        ),
        check_vma=False,
    )
```
